128 devices in a mesh: span: 8 (over x_lo, y), seq: 16 (over x_hi, z, core).
Axes of the slice: x: 4 (x_hi: 2, x_lo: 2; x = x_hi * 2 + x_lo), y: 4, z: 4, core: 2. Of those that a mesh axis runs over, the one named last changes fastest.
Arguments:
- latent: bfloat16 [8, 1024, 5120], P('span', 'seq'), may hold values from -6 to 6
- noise: bfloat16 [8, 1024, 5120], P('span', 'seq'), may hold values from -6 to 6
- clean_keys: bfloat16 [8, 1024, 4096], P('span', None, 'seq'), may hold values from -256 to 256
- clean_values: bfloat16 [8, 1024, 4096], P('span', None, 'seq'), may hold values from -6 to 6
- w_query: bfloat16 [5120, 4096], P(None, 'seq'), may hold values from -0.078125 to 0.078125
- w_key: bfloat16 [5120, 4096], P(None, 'seq'), may hold values from -0.078125 to 0.078125
- w_value: bfloat16 [5120, 4096], P(None, 'seq'), may hold values from -0.078125 to 0.078125
- w_out: bfloat16 [4096, 5120], P('seq'), may hold values from -1.5 to 1.5
- modulation: float32 [8, 2, 5120], replicated, may hold values from -2 to 2
- plan: float32 [8, 2], replicated, may hold values from 0.15 to 1, as said below
- step_index: int32 [8], replicated, may hold values from 0 to 7
- assignment: int32 [8], replicated, may hold values from 0 to 7, each once
- visible: int32 [8, 8], replicated, may hold values from 0 to 1, as said below
Outputs:
- renoised: bfloat16 [8, 1024, 5120], P('span', 'seq')
The draws below stay inside these ranges and needn't reach their ends.
Inputs may be any that keep to these rules, and one draw needn't show every extreme that they name: visible[c, j] is 1 only where j < c, and the row of span 8 - 1 is 1 at every j < 7. plan[i, 1] lies below plan[i, 0].
All inputs are finite; a program needn't handle non-finite values.
Results may differ from the reference program's by a relative error of at most 0.02.
Values may be sent and summed in bfloat16 or wider, within the bound.
A program may use at most 192 MiB of HBM per device.

```python
import jax
import jax.numpy as jnp
from jax import lax

D = 5120
HD = 128
HEADS = 32
STEPS = 8
INNER = 4096
CTOK = 1024
SPANS = 8
N_SEQ = 16


def draw_clean_keys(key, part):
    key = jax.random.fold_in(key, 11)
    base_key = jax.random.fold_in(key, 0)
    values = jnp.clip(jax.random.normal(base_key, (SPANS, CTOK, INNER), jnp.float32), -6.0, 6.0)
    return values.astype(jnp.bfloat16)


def draw_plan(key, part):
    key = jax.random.fold_in(key, 23)
    first_key, second_key = jax.random.split(key)
    level_now = jax.random.uniform(first_key, (STEPS,), jnp.float32, 0.5, 1.0)
    level_next = level_now * jax.random.uniform(second_key, (STEPS,), jnp.float32, 0.3, 0.8)
    return jnp.stack([level_now, level_next], axis=1)


def draw_visible(key, part):
    key = jax.random.fold_in(key, 37)
    picks = jax.random.randint(key, (SPANS, SPANS), 0, 4)
    rows = jnp.arange(SPANS, dtype=jnp.int32)[:, None]
    cols = jnp.arange(SPANS, dtype=jnp.int32)[None, :]
    lower = cols < rows
    chosen = jnp.logical_or(picks > 0, rows == SPANS - 1)
    return jnp.logical_and(lower, chosen).astype(jnp.int32)


def with_ends(values, stream_key, low, largest):
    shape = values.shape
    spot = [jax.random.randint(jax.random.fold_in(stream_key, axis), (), 0, shape[axis]) for axis in range(len(shape))]
    values = values.at[tuple(spot)].set(low)
    longest = shape.index(max(shape))
    spot[longest] = (spot[longest] + 1) % shape[longest]
    return values.at[tuple(spot)].set(largest)


def block_levels(rng, dims, shards, low, largest):
    level, own = 1.0, jax.random.fold_in(rng, 6)
    for axis_at, blocks in shards:
        heights = jnp.exp(jax.random.uniform(jax.random.fold_in(own, axis_at), (blocks,), jnp.float32, low / len(shards), largest / len(shards)))
        level = level * jnp.repeat(heights, dims[axis_at] // blocks).reshape([-1 if axis == axis_at else 1 for axis in range(len(dims))])
    return level


def normal_values(key, shape, spread, limit, pieces=(), kind=jnp.bfloat16):
    values = spread * jax.random.normal(key, shape, jnp.float32)
    if pieces:
        values = values * block_levels(key, shape, pieces, -0.22, 0.18)
    return jnp.clip(values, -limit, limit).astype(kind)


def setup_inputs(seed: int = 0) -> dict:
    splits = jax.random.split(jax.random.key(seed), 14)
    return {
        "latent": normal_values(splits[0], (SPANS, CTOK, D), 1.0, 6.0, ((0, 8), (1, 16))),
        "noise": normal_values(splits[1], (SPANS, CTOK, D), 1.0, 6.0, ((0, 8), (1, 16))),
        "clean_keys": draw_clean_keys(jax.random.fold_in(splits[13], 71), 0),
        "clean_values": normal_values(splits[3], (SPANS, CTOK, INNER), 1.0, 6.0, ((0, 8), (2, 16))),
        "w_query": normal_values(splits[4], (D, INNER), D ** -0.5, 0.078125, ((1, 16),)),
        "w_key": normal_values(splits[5], (D, INNER), D ** -0.5, 0.078125, ((1, 16),)),
        "w_value": normal_values(splits[6], (D, INNER), D ** -0.5, 0.078125, ((1, 16),)),
        "w_out": normal_values(splits[7], (INNER, D), (INNER // 256) ** -0.5, 1.5, ((0, 16),)),
        "modulation": normal_values(splits[8], (STEPS, 2, D), 0.3, 2.0, (), jnp.float32),
        "plan": draw_plan(jax.random.fold_in(splits[13], 71), 0),
        "step_index": with_ends(jax.random.randint(splits[10], (SPANS,), 0, STEPS), jax.random.fold_in(splits[10], 1), 0, STEPS - 1).astype(jnp.int32),
        "assignment": jax.random.permutation(splits[11], SPANS).astype(jnp.int32),
        "visible": draw_visible(jax.random.fold_in(splits[13], 71), 0),
    }


def reference(latent, noise, clean_keys, clean_values, w_query, w_key, w_value, w_out, modulation, plan, step_index, assignment, visible):
    factor = 1.0 / HD ** 0.5
    block = INNER // N_SEQ
    span_mask = visible[assignment][:, assignment].astype(jnp.float32)
    all_keys = clean_keys.reshape(SPANS * CTOK, INNER)
    all_values = clean_values.reshape(SPANS * CTOK, INNER)

    def one_group(group):
        xrows = latent[group].astype(jnp.float32)
        entry = step_index[group]
        shift = modulation[entry, 0]
        scale = modulation[entry, 1]
        level_now = plan[entry, 0]
        level_next = plan[entry, 1]
        rms = lax.rsqrt(lax.optimization_barrier(jnp.mean(xrows * xrows, axis=1, keepdims=True)) + 1e-06)
        normed = (xrows * rms * (1.0 + scale) + shift).astype(jnp.bfloat16)
        query = jnp.dot(normed, w_query, preferred_element_type=jnp.float32).astype(jnp.bfloat16)
        keys = jnp.dot(normed, w_key, preferred_element_type=jnp.float32).astype(jnp.bfloat16)
        values = jnp.dot(normed, w_value, preferred_element_type=jnp.float32).astype(jnp.bfloat16)
        key_mask = jnp.repeat(span_mask[group], CTOK)

        def head(index):
            start = index * HD
            qh = lax.dynamic_slice_in_dim(query, start, HD, 1)
            kh = lax.dynamic_slice_in_dim(keys, start, HD, 1)
            vh = lax.dynamic_slice_in_dim(values, start, HD, 1)
            ck = lax.dynamic_slice_in_dim(all_keys, start, HD, 1)
            cv = lax.dynamic_slice_in_dim(all_values, start, HD, 1)
            own = jnp.dot(qh, kh.T, preferred_element_type=jnp.float32) * factor
            far = jnp.dot(qh, ck.T, preferred_element_type=jnp.float32) * factor
            far = jnp.where(key_mask[None, :] > 0, far, -jnp.inf)
            top = jnp.maximum(lax.optimization_barrier(jnp.max(own, axis=1)), lax.optimization_barrier(jnp.max(far, axis=1)))
            p_own = jnp.exp(own - top[:, None]).astype(jnp.bfloat16)
            p_far = jnp.exp(far - top[:, None]).astype(jnp.bfloat16)
            total = lax.optimization_barrier(jnp.sum(p_own.astype(jnp.float32), axis=1)) + lax.optimization_barrier(jnp.sum(p_far.astype(jnp.float32), axis=1))
            acc = jnp.dot(p_own, vh, preferred_element_type=jnp.float32) + jnp.dot(p_far, cv, preferred_element_type=jnp.float32)
            return acc / total[:, None]
        heads_out = lax.map(head, jnp.arange(HEADS, dtype=jnp.int32))
        attended = jnp.transpose(heads_out, (1, 0, 2)).reshape(CTOK, INNER).astype(jnp.bfloat16)

        def add_block(index, summed):
            start = index * block
            piece = lax.dynamic_slice_in_dim(attended, start, block, 1)
            weight = lax.dynamic_slice_in_dim(w_out, start, block, 0)
            partial_value = jnp.dot(piece, weight, preferred_element_type=jnp.float32).astype(jnp.bfloat16)
            return summed + partial_value.astype(jnp.float32)
        mixed = lax.fori_loop(0, N_SEQ, add_block, jnp.zeros((CTOK, D), jnp.float32))
        result = (1.0 - level_next) * (xrows - level_now * (xrows + mixed)) + level_next * noise[group].astype(jnp.float32)
        return result.astype(jnp.bfloat16)
    return lax.map(one_group, jnp.arange(SPANS, dtype=jnp.int32))
```

```python
import jax
import jax.numpy as jnp
from jax import lax
from jax.experimental import pallas as pl
from jax.experimental.pallas import tpu as pltpu
from jax.sharding import PartitionSpec as P

HD = 128
D = 5120
TOK = 1024
W = 256
ROWS = 64
HALF = 32
GROUP = 256
PIECE = 256
LOG2E = 1.4426950408889634
SCALE = LOG2E / HD**0.5
LOW = -1e30
HIGH = 3e38
MESH = pl.DeviceIdType.MESH
N_SEM = 144

PLACE = {(0, 0): 0, (1, 0): 1, (0, 1): 2, (0, 3): 3, (1, 1): 4, (1, 3): 5, (0, 2): 6, (1, 2): 7}
CACHE = {(0, 0): 0, (0, 1): 1, (0, 3): 2, (1, 0): 3, (1, 1): 4, (1, 3): 5, (0, 2): 6, (1, 2): 7}
OWN = 8
A, B, C, E = 0, 1, 2, 3


def kernel(
    latent_hbm,
    noise_hbm,
    ck_hbm,
    cv_hbm,
    wq_hbm,
    wk_hbm,
    wv_hbm,
    wo_hbm,
    modulation,
    plan,
    step_index,
    assignment,
    visible,
    out,
    lat,
    noise,
    w,
    wo,
    g,
    kv,
    q,
    acc,
    top,
    att,
    p0,
    p1,
    s,
    r1,
    r2,
    xb,
    flags,
    local_sem,
    send_sem,
    recv_sem,
):
    span = lax.axis_index("span")
    seq = lax.axis_index("seq")
    x_lo = span // 4
    y = span % 4
    x_hi = seq // 8
    z = (seq // 2) % 4
    core = seq % 2

    def seq_of(a, b, c):
        return a * 8 + b * 2 + c

    sib = (span, seq_of(x_hi, z, 1 - core))
    x2 = (span, seq_of(1 - x_hi, z, core))
    zp = (span, seq_of(x_hi, (z + 1) % 4, core))
    zm = (span, seq_of(x_hi, (z + 3) % 4, core))
    xn = ((1 - x_lo) * 4 + y, seq)
    yp = (x_lo * 4 + (y + 1) % 4, seq)
    ym = (x_lo * 4 + (y + 3) % 4, seq)

    loads = {}
    for i, (name, src, dst) in enumerate(
        (
            ("k", ck_hbm.at[0], kv.at[0, 0]),
            ("v", cv_hbm.at[0], kv.at[0, 1]),
            ("lat", latent_hbm.at[0], lat),
            ("wq", wq_hbm, w.at[0]),
            ("wk", wk_hbm, w.at[1]),
            ("wv", wv_hbm, w.at[2]),
            ("wo", wo_hbm, wo),
            ("noise", noise_hbm.at[0], noise),
        )
    ):
        loads[name] = pltpu.make_async_copy(src, dst, local_sem.at[i])
        loads[name].start()

    barrier = pltpu.get_barrier_semaphore()
    for device in (sib, x2, zp, zm, xn, yp, ym):
        pl.semaphore_signal(barrier, 1, device_id=device, device_id_type=MESH)
    pl.semaphore_wait(barrier, 7)

    started = []

    def send(src, dst, device):
        i = len(started)
        copy = pltpu.make_async_remote_copy(
            src, dst, send_sem.at[i], recv_sem.at[i], device_id=device, device_id_type=MESH
        )
        copy.start()
        started.append(copy)
        return copy

    def piece(place, j):
        return kv.at[place, :, pl.ds(j * PIECE, PIECE)]

    def part(place, side, j):
        return kv.at[place, side, pl.ds(j * PIECE, PIECE)]

    def send_piece(src, dst, j, device):
        return send(piece(CACHE[src], j), piece(CACHE[dst], j), device)

    loads["k"].wait()
    loads["v"].wait()
    y_up, y_down, x_over = {}, {}, {}
    for j in range(4):
        y_up[0, j] = send_piece((0, 0), (0, 3), j, yp)
        y_down[0, j] = send_piece((0, 0), (0, 1), j, ym)
    x_over[0, 0] = send_piece((0, 0), (1, 0), 0, xn)

    def rows_of(place, sub, half=None):
        base = PLACE[place] * 2 * ROWS + sub * ROWS
        if half is None:
            return g.at[pl.ds(base, ROWS)]
        return g.at[pl.ds(base + half * HALF, HALF)]

    step = step_index[span]
    level_now = plan[step, 0]
    level_next = plan[step, 1]
    loads["lat"].wait()

    @pl.loop(0, 4)
    def _(i):
        rows = pl.ds(pl.multiple_of(i * 16, 16), 16)
        values = lat[rows, :].astype(jnp.float32)
        rms = lax.rsqrt(jnp.mean(values * values, axis=1, keepdims=True) + 1e-06)
        shift = modulation[step, 0:1, :]
        scale = modulation[step, 1:2, :]
        g[rows, :] = (values * rms * (1.0 + scale) + shift).astype(jnp.bfloat16)

    x_part, z_up, z_down, over = {}, {}, {}, {}
    for h in range(2):
        x_part[h] = send(rows_of((0, 0), 0, h), rows_of((1, 0), 0, h), x2)
    for h in range(2):
        z_up[0, h] = send(rows_of((0, 0), 0, h), rows_of((0, 3), 0, h), zp)
        z_down[0, h] = send(rows_of((0, 0), 0, h), rows_of((0, 1), 0, h), zm)

    def to_sibling(place):
        over[place] = send(rows_of(place, 0), rows_of(place, 1), sib)

    to_sibling((0, 0))

    mine = assignment[span]
    for (dx, dy), place in CACHE.items():
        other = ((x_lo + dx) % 2) * 4 + (y + dy) % 4
        flags[place] = visible[mine, assignment[other]]
    flags[OWN] = 1

    acc[...] = jnp.zeros_like(acc)
    top[...] = jnp.full_like(top, LOW)

    for h in range(2):
        x_part[h].wait_recv()
        z_up[1, h] = send(rows_of((1, 0), 0, h), rows_of((1, 3), 0, h), zp)
        z_down[1, h] = send(rows_of((1, 0), 0, h), rows_of((1, 1), 0, h), zm)
    to_sibling((1, 0))
    for j in (1, 2):
        x_over[0, j] = send_piece((0, 0), (1, 0), j, xn)

    def project(group):
        rows = pl.ds(group * GROUP, GROUP)

        @pl.loop(0, 3)
        def _(i):
            y = jnp.dot(g[rows, :], w[i], preferred_element_type=jnp.float32).astype(jnp.bfloat16)

            @pl.when(i == 0)
            def _():
                q[rows, :] = y

            @pl.when(i > 0)
            def _():
                kv[OWN, i - 1, rows, :] = y

    ones = jnp.ones((TOK, HD), jnp.bfloat16)

    def attend(group, place):
        rows = pl.ds(pl.multiple_of(group * GROUP, GROUP), GROUP)
        seen = jnp.full((GROUP, HD), flags[place], jnp.int32) > 0
        for h in range(W // HD):
            cols = slice(h * HD, (h + 1) * HD)
            scores = lax.dot_general(
                q[rows, cols],
                kv[place, 0, :, cols],
                (((1,), (1,)), ((), ())),
                preferred_element_type=jnp.float32,
            )
            old = top[rows, cols]
            peak = jnp.max(scores, axis=1, keepdims=True) * SCALE
            new = jnp.where(seen, jnp.maximum(old, peak), old)
            low = jnp.where(seen, new, HIGH)
            weights = jnp.exp2(scores * SCALE - jnp.tile(low, (1, TOK // HD))).astype(jnp.bfloat16)
            both = jnp.concatenate((kv[place, 1, :, cols], ones), axis=1)
            sums = jnp.dot(weights, both, preferred_element_type=jnp.float32)
            shrink = jnp.exp2(old - new)
            wide = slice(h * 2 * HD, (h + 1) * 2 * HD)
            acc[rows, wide] = acc[rows, wide] * jnp.tile(shrink, (1, 2)) + sums
            top[rows, cols] = new

    def attend_all(first_group, last_group, first_place, last_place):
        groups = last_group - first_group + 1

        @pl.loop(0, groups * (last_place - first_place + 1))
        def _(i):
            attend(first_group + i % groups, first_place + i // groups)

    for name in ("wq", "wk", "wv"):
        loads[name].wait()
    x_over[0, 0].wait_recv()
    y_up[1, 0] = send_piece((1, 0), (1, 3), 0, yp)
    y_down[1, 0] = send_piece((1, 0), (1, 1), 0, ym)
    over[0, 0].wait_recv()
    over[1, 0].wait_recv()
    project(A)

    z_fwd_up, z_fwd_down = {}, {}

    def forward_z(x):
        for h in range(2):
            z_up[x, h].wait_recv()
            z_down[x, h].wait_recv()
        z_fwd_up[x] = send(rows_of((x, 3), 0, 0), rows_of((x, 2), 0, 0), zp)
        z_fwd_down[x] = send(rows_of((x, 1), 0, 1), rows_of((x, 2), 0, 1), zm)
        to_sibling((x, 3))
        to_sibling((x, 1))

    forward_z(0)
    over[0, 1].wait_recv()
    over[0, 3].wait_recv()
    project(B)
    attend_all(A, B, 0, 0)
    for j in range(4):
        y_up[0, j].wait_recv()
        y_down[0, j].wait_recv()
    attend_all(A, B, 1, 2)
    forward_z(1)
    for j in (1, 2):
        x_over[0, j].wait_recv()
        y_up[1, j] = send_piece((1, 0), (1, 3), j, yp)
        y_down[1, j] = send_piece((1, 0), (1, 1), j, ym)
    y_fwd_up, y_fwd_down = {}, {}

    def forward_y(x, j):
        y_fwd_up[x, j] = send(part(CACHE[x, 3], 0, j), part(CACHE[x, 2], 0, j), yp)
        y_fwd_down[x, j] = send(part(CACHE[x, 1], 1, j), part(CACHE[x, 2], 1, j), ym)

    for j in (3, 0, 1, 2):
        forward_y(0, j)
    for dy in (0, 1, 3):
        x_over[dy, 3] = send_piece((0, dy), (1, dy), 3, xn)
    over[1, 1].wait_recv()
    over[1, 3].wait_recv()
    project(C)
    attend_all(C, C, 0, 2)
    for x in range(2):
        z_fwd_up[x].wait_recv()
        z_fwd_down[x].wait_recv()
        to_sibling((x, 2))
    x_over[0, 3].wait_recv()
    attend_all(A, C, 3, 3)
    for j in range(3):
        y_up[1, j].wait_recv()
        y_down[1, j].wait_recv()
        forward_y(1, j)
    y_fwd_up[0, 3].wait_recv()
    y_fwd_down[0, 3].wait_recv()
    x_over[2, 3] = send_piece((0, 2), (1, 2), 3, xn)
    over[0, 2].wait_recv()
    over[1, 2].wait_recv()
    project(E)
    attend_all(E, E, 0, 3)
    attend_all(A, E, OWN, OWN)
    x_over[1, 3].wait_recv()
    x_over[3, 3].wait_recv()
    attend_all(A, E, 4, 5)
    for j in range(3):
        y_fwd_up[0, j].wait_recv()
        y_fwd_down[0, j].wait_recv()
    for j in range(3):
        y_fwd_up[1, j].wait_recv()
        y_fwd_down[1, j].wait_recv()
    x_over[2, 3].wait_recv()
    loads["wo"].wait()
    loads["noise"].wait()

    part_over = {}

    def finish(group):
        attend_all(group, group, 6, 7)
        rows = pl.ds(group * GROUP, GROUP)
        for h in range(W // HD):
            lead = h * 2 * HD
            att[:, h * HD : (h + 1) * HD] = (
                acc[rows, lead : lead + HD] / acc[rows, lead + HD : lead + 2 * HD]
            ).astype(jnp.bfloat16)

        @pl.loop(0, 10)
        def _(i):
            cols = pl.ds(pl.multiple_of(i * 512, 512), 512)
            y = jnp.dot(att[...], wo[:, cols], preferred_element_type=jnp.float32)
            y = y.astype(jnp.bfloat16)
            p0[2 * group, :, cols] = y[:ROWS]
            p1[2 * group, :, cols] = y[ROWS : 2 * ROWS]
            p0[2 * group + 1, :, cols] = y[2 * ROWS : 3 * ROWS]
            p1[2 * group + 1, :, cols] = y[3 * ROWS :]

        for place in (2 * group + 1, 2 * group):
            part_over[place] = send(p1.at[place], s.at[place], sib)

    def total(dst, *terms):
        count = dst.shape[0] // 16

        @pl.loop(0, count)
        def _(i):
            rows = pl.ds(pl.multiple_of(i * 16, 16), 16)
            value = terms[0][rows, :].astype(jnp.float32)
            for term in terms[1:]:
                value = value + term[rows, :].astype(jnp.float32)
            dst[rows, :] = value.astype(jnp.bfloat16)

    half_rows = (pl.ds(0, HALF), pl.ds(HALF, HALF))
    r1_up, r1_down, r2_up, r2_down = {}, {}, {}, {}

    def first_hop(x):
        place = PLACE[x, 2]
        part_over[place].wait_recv()
        total(p0.at[place], p0.at[place], s.at[place])
        r1_up[x] = send(p0.at[place, half_rows[0]], r1.at[x, 0], zp)
        r1_down[x] = send(p0.at[place, half_rows[1]], r1.at[x, 1], zm)

    def second_hop(x):
        up, down = PLACE[x, 1], PLACE[x, 3]
        part_over[up].wait_recv()
        part_over[down].wait_recv()
        a, b = half_rows
        total(p0.at[up, b], p0.at[up, b], s.at[up, b])
        r2_up[x, 1] = send(p0.at[up, b], r2.at[x, 0, b], zp)
        total(p0.at[down, a], p0.at[down, a], s.at[down, a])
        r2_down[x, 0] = send(p0.at[down, a], r2.at[x, 1, a], zm)
        r1_up[x].wait_recv()
        total(p0.at[up, a], p0.at[up, a], s.at[up, a], r1.at[x, 0])
        r2_up[x, 0] = send(p0.at[up, a], r2.at[x, 0, a], zp)
        r1_down[x].wait_recv()
        total(p0.at[down, b], p0.at[down, b], s.at[down, b], r1.at[x, 1])
        r2_down[x, 1] = send(p0.at[down, b], r2.at[x, 1, b], zm)

    finish(E)
    finish(C)
    first_hop(1)
    first_hop(0)
    finish(B)
    finish(A)
    second_hop(1)
    second_hop(0)
    part_over[1].wait_recv()
    last = {}
    for h, rows in ((0, half_rows[0]), (1, half_rows[1])):
        r2_up[1, h].wait_recv()
        r2_down[1, h].wait_recv()
        total(p0.at[1, rows], p0.at[1, rows], s.at[1, rows], r2.at[1, 0, rows], r2.at[1, 1, rows])
        last[h] = send(p0.at[1, rows], xb.at[rows], x2)
    part_over[0].wait_recv()
    for h in range(2):
        r2_up[0, h].wait_recv()
        r2_down[0, h].wait_recv()
        last[h].wait_recv()

    @pl.loop(0, 4)
    def _(i):
        rows = pl.ds(pl.multiple_of(i * 16, 16), 16)
        mixed = p0[0, rows, :].astype(jnp.float32) + s[0, rows, :].astype(jnp.float32)
        mixed = mixed + r2[0, 0, rows, :].astype(jnp.float32) + r2[0, 1, rows, :].astype(jnp.float32)
        mixed = mixed + xb[rows, :].astype(jnp.float32)
        xrows = lat[rows, :].astype(jnp.float32)
        fresh = noise[rows, :].astype(jnp.float32)
        result = (1.0 - level_next) * (xrows - level_now * (xrows + mixed)) + level_next * fresh
        out[0, rows, :] = result.astype(jnp.bfloat16)

    for copy in started:
        copy.wait_send()


def local(*operands):
    bf16, f32 = jnp.bfloat16, jnp.float32
    anywhere = pl.BlockSpec(memory_space=pl.ANY)
    vmem = pl.BlockSpec(memory_space=pltpu.VMEM)
    smem = pl.BlockSpec(memory_space=pltpu.SMEM)
    return pl.pallas_call(
        kernel,
        out_shape=jax.ShapeDtypeStruct((1, ROWS, D), bf16),
        in_specs=[anywhere] * 8 + [vmem] + [smem] * 4,
        out_specs=vmem,
        scratch_shapes=[
            pltpu.VMEM((ROWS, D), bf16),
            pltpu.VMEM((ROWS, D), bf16),
            pltpu.VMEM((3, D, W), bf16),
            pltpu.VMEM((W, D), bf16),
            pltpu.VMEM((TOK, D), bf16),
            pltpu.VMEM((9, 2, TOK, W), bf16),
            pltpu.VMEM((TOK, W), bf16),
            pltpu.VMEM((TOK, 2 * W), f32),
            pltpu.VMEM((TOK, W), f32),
            pltpu.VMEM((GROUP, W), bf16),
            pltpu.VMEM((8, ROWS, D), bf16),
            pltpu.VMEM((8, ROWS, D), bf16),
            pltpu.VMEM((8, ROWS, D), bf16),
            pltpu.VMEM((2, 2, HALF, D), bf16),
            pltpu.VMEM((2, 2, ROWS, D), bf16),
            pltpu.VMEM((ROWS, D), bf16),
            pltpu.SMEM((16,), jnp.int32),
            pltpu.SemaphoreType.DMA((8,)),
            pltpu.SemaphoreType.DMA((N_SEM,)),
            pltpu.SemaphoreType.DMA((N_SEM,)),
        ],
        compiler_params=pltpu.CompilerParams(
            collective_id=0, has_side_effects=True, vmem_limit_bytes=62 * 2**20
        ),
    )(*operands)


def solution(mesh):
    in_specs = (
        P("span", "seq", None),
        P("span", "seq", None),
        P("span", None, "seq"),
        P("span", None, "seq"),
        P(None, "seq"),
        P(None, "seq"),
        P(None, "seq"),
        P("seq", None),
        P(),
        P(),
        P(),
        P(),
        P(),
    )
    out_specs = P("span", "seq", None)
    return jax.shard_map(local, mesh=mesh, in_specs=in_specs, out_specs=out_specs, check_vma=False)
```

```python
import itertools

import jax
import jax.numpy as jnp
from jax import lax
from jax.experimental import pallas as pl
from jax.experimental.pallas import tpu as pltpu
from jax.sharding import PartitionSpec as P

HD = 128
D = 5120
TOK = 1024
W = 256
ROWS = 64
HALF = 32
GROUP = 256
PIECE = 256
LOG2E = 1.4426950408889634
SCALE = LOG2E / HD**0.5
LOW = -1e30
HIGH = 3e38
MESH = pl.DeviceIdType.MESH
N_SEM = 144

PLACE = {(0, 0): 0, (1, 0): 1, (0, 1): 2, (0, 3): 3, (1, 1): 4, (1, 3): 5, (0, 2): 6, (1, 2): 7}
CACHE = {(0, 0): 0, (0, 1): 1, (0, 3): 2, (1, 0): 3, (1, 1): 4, (1, 3): 5, (0, 2): 6, (1, 2): 7}
OWN = 8
A, B, C, E = 0, 1, 2, 3


def kernel(
    latent_hbm,
    noise_hbm,
    ck_hbm,
    cv_hbm,
    wq_hbm,
    wk_hbm,
    wv_hbm,
    wo_hbm,
    modulation,
    plan,
    step_index,
    assignment,
    visible,
    out,
    lat,
    noise,
    w,
    wo,
    g,
    kv,
    q,
    acc,
    top,
    att,
    s,
    r1,
    r2,
    xf,
    xb,
    flags,
    local_sem,
    send_sem,
    recv_sem,
):
    span = lax.axis_index("span")
    seq = lax.axis_index("seq")
    x_lo = span // 4
    y = span % 4
    x_hi = seq // 8
    z = (seq // 2) % 4
    core = seq % 2

    def seq_of(a, b, c):
        return a * 8 + b * 2 + c

    sib = (span, seq_of(x_hi, z, 1 - core))
    x2 = (span, seq_of(1 - x_hi, z, core))
    zp = (span, seq_of(x_hi, (z + 1) % 4, core))
    zm = (span, seq_of(x_hi, (z + 3) % 4, core))
    xn = ((1 - x_lo) * 4 + y, seq)
    yp = (x_lo * 4 + (y + 1) % 4, seq)
    ym = (x_lo * 4 + (y + 3) % 4, seq)

    loads = {}
    for i, (name, src, dst) in enumerate(
        (
            ("k", ck_hbm.at[0], kv.at[0, 0]),
            ("v", cv_hbm.at[0], kv.at[0, 1]),
            ("lat", latent_hbm.at[0], lat),
            ("wq", wq_hbm, w.at[0]),
            ("wk", wk_hbm, w.at[1]),
            ("wv", wv_hbm, w.at[2]),
            ("wo", wo_hbm, wo),
            ("noise", noise_hbm.at[0], noise),
        )
    ):
        loads[name] = pltpu.make_async_copy(src, dst, local_sem.at[i])
        loads[name].start()

    barrier = pltpu.get_barrier_semaphore()
    for device in (sib, x2, zp, zm, xn, yp, ym):
        pl.semaphore_signal(barrier, 1, device_id=device, device_id_type=MESH)
    pl.semaphore_wait(barrier, 7)

    started = []
    count = itertools.count()

    def send(src, dst, device):
        i = next(count)
        copy = pltpu.make_async_remote_copy(
            src, dst, send_sem.at[i], recv_sem.at[i], device_id=device, device_id_type=MESH
        )
        copy.start()
        started.append(copy)
        return copy

    def piece(place, j):
        return kv.at[place, :, pl.ds(j * PIECE, PIECE)]

    def part(place, side, j):
        return kv.at[place, side, pl.ds(j * PIECE, PIECE)]

    def send_piece(src, dst, j, device):
        return send(piece(CACHE[src], j), piece(CACHE[dst], j), device)

    loads["k"].wait()
    loads["v"].wait()
    y_up, y_down, x_over = {}, {}, {}
    for j in range(4):
        y_up[0, j] = send_piece((0, 0), (0, 3), j, yp)
        y_down[0, j] = send_piece((0, 0), (0, 1), j, ym)
    x_over[0, 0] = send_piece((0, 0), (1, 0), 0, xn)

    def rows_of(place, sub, half=None):
        base = PLACE[place] * 2 * ROWS + sub * ROWS
        if half is None:
            return g.at[pl.ds(base, ROWS)]
        return g.at[pl.ds(base + half * HALF, HALF)]

    step = step_index[span]
    level_now = plan[0, step]
    level_next = plan[1, step]
    loads["lat"].wait()

    @pl.loop(0, 4)
    def _(i):
        rows = pl.ds(pl.multiple_of(i * 16, 16), 16)
        values = lat[rows, :].astype(jnp.float32)
        rms = lax.rsqrt(jnp.mean(values * values, axis=1, keepdims=True) + 1e-06)
        shift = modulation[step, 0:1, :]
        scale = modulation[step, 1:2, :]
        g[rows, :] = (values * rms * (1.0 + scale) + shift).astype(jnp.bfloat16)

    x_part, z_up, z_down, over = {}, {}, {}, {}
    for h in range(2):
        x_part[h] = send(rows_of((0, 0), 0, h), rows_of((1, 0), 0, h), x2)
    for h in range(2):
        z_up[0, h] = send(rows_of((0, 0), 0, h), rows_of((0, 3), 0, h), zp)
        z_down[0, h] = send(rows_of((0, 0), 0, h), rows_of((0, 1), 0, h), zm)

    def to_sibling(place):
        over[place] = send(rows_of(place, 0), rows_of(place, 1), sib)

    to_sibling((0, 0))

    mine = assignment[span]
    for (dx, dy), place in CACHE.items():
        other = ((x_lo + dx) % 2) * 4 + (y + dy) % 4
        flags[place] = visible[mine, assignment[other]]
    flags[OWN] = 1

    acc[...] = jnp.zeros_like(acc)
    top[...] = jnp.full_like(top, LOW)

    for h in range(2):
        x_part[h].wait_recv()
        z_up[1, h] = send(rows_of((1, 0), 0, h), rows_of((1, 3), 0, h), zp)
        z_down[1, h] = send(rows_of((1, 0), 0, h), rows_of((1, 1), 0, h), zm)
    to_sibling((1, 0))
    for j in (1, 2):
        x_over[0, j] = send_piece((0, 0), (1, 0), j, xn)

    def project(group):
        rows = pl.ds(group * GROUP, GROUP)

        @pl.loop(0, 3)
        def _(i):
            y = jnp.dot(g[rows, :], w[i], preferred_element_type=jnp.float32)
            y = (y * jnp.where(i == 0, SCALE, 1.0)).astype(jnp.bfloat16)

            @pl.when(i == 0)
            def _():
                q[rows, :] = y

            @pl.when(i > 0)
            def _():
                kv[OWN, i - 1, rows, :] = y

    ones = jnp.ones((TOK, HD), jnp.bfloat16)

    def attend(groups, places):
        items = [(pl.ds(pl.multiple_of(i * GROUP, GROUP), GROUP), h) for i in groups for h in range(W // HD)]
        seen = [jnp.full((GROUP, HD), flags[place], jnp.int32) > 0 for place in places]
        olds = [top[rows, h * HD : (h + 1) * HD] for rows, h in items]
        scores, results = {}, {}

        def score(i):
            rows, h = items[i]
            cols = slice(h * HD, (h + 1) * HD)
            scores[i] = [
                lax.dot_general(
                    q[rows, cols],
                    kv[place, 0, :, cols],
                    (((1,), (1,)), ((), ())),
                    preferred_element_type=jnp.float32,
                )
                for place in places
            ]

        def weigh(i):
            rows, h = items[i]
            cols = slice(h * HD, (h + 1) * HD)
            new = olds[i]
            for mark, block in zip(seen, scores[i]):
                new = jnp.where(mark, jnp.maximum(new, jnp.max(block, axis=1, keepdims=True)), new)
            shrink = jnp.exp2(olds[i] - new)
            lead = h * 2 * HD
            value = acc[rows, lead : lead + HD] * shrink
            total = acc[rows, lead + HD : lead + 2 * HD] * shrink
            for mark, block, place in zip(seen, scores[i], places):
                low = jnp.where(mark, new, HIGH)
                weights = jnp.exp2(block - jnp.tile(low, (1, TOK // HD))).astype(jnp.bfloat16)
                both = jnp.concatenate((kv[place, 1, :, cols], ones), axis=1)
                sums = jnp.dot(weights, both, preferred_element_type=jnp.float32)
                value = value + sums[:, :HD]
                total = total + sums[:, HD:]
            results[i] = (new, value, total)

        score(0)
        for i in range(len(items)):
            if i + 1 < len(items):
                score(i + 1)
            weigh(i)
        for i, (rows, h) in enumerate(items):
            lead = h * 2 * HD
            top[rows, h * HD : (h + 1) * HD], acc[rows, lead : lead + HD], acc[rows, lead + HD : lead + 2 * HD] = (
                results[i]
            )

    for name in ("wq", "wk", "wv"):
        loads[name].wait()
    x_over[0, 0].wait_recv()
    y_up[1, 0] = send_piece((1, 0), (1, 3), 0, yp)
    y_down[1, 0] = send_piece((1, 0), (1, 1), 0, ym)
    over[0, 0].wait_recv()
    over[1, 0].wait_recv()
    project(A)

    z_fwd_up, z_fwd_down = {}, {}

    def forward_z(x):
        for h in range(2):
            z_up[x, h].wait_recv()
            z_down[x, h].wait_recv()
        z_fwd_up[x] = send(rows_of((x, 3), 0, 0), rows_of((x, 2), 0, 0), zp)
        z_fwd_down[x] = send(rows_of((x, 1), 0, 1), rows_of((x, 2), 0, 1), zm)
        to_sibling((x, 3))
        to_sibling((x, 1))

    y_fwd_up, y_fwd_down = {}, {}

    def forward_y(x, j):
        y_fwd_up[x, j] = send(part(CACHE[x, 3], 0, j), part(CACHE[x, 2], 0, j), yp)
        y_fwd_down[x, j] = send(part(CACHE[x, 1], 1, j), part(CACHE[x, 2], 1, j), ym)

    forward_z(0)
    over[0, 1].wait_recv()
    over[0, 3].wait_recv()
    project(B)
    attend([A, B], [0])
    for j in range(4):
        y_up[0, j].wait_recv()
        y_down[0, j].wait_recv()
    x_over[0, 1].wait_recv()
    y_up[1, 1] = send_piece((1, 0), (1, 3), 1, yp)
    y_down[1, 1] = send_piece((1, 0), (1, 1), 1, ym)

    @pl.loop(1, 3)
    def _(place):
        attend([A, B], [place])

    forward_z(1)
    x_over[0, 2].wait_recv()
    y_up[1, 2] = send_piece((1, 0), (1, 3), 2, yp)
    y_down[1, 2] = send_piece((1, 0), (1, 1), 2, ym)
    for j in (3, 0, 1, 2):
        forward_y(0, j)
    for dy in (0, 1, 3):
        x_over[dy, 3] = send_piece((0, dy), (1, dy), 3, xn)
    over[1, 1].wait_recv()
    over[1, 3].wait_recv()
    project(C)
    attend([C], [0, 1])
    z_fwd_up[0].wait_recv()
    z_fwd_down[0].wait_recv()
    to_sibling((0, 2))
    x_over[0, 3].wait_recv()
    attend([A, B], [3])
    for j in range(3):
        y_up[1, j].wait_recv()
        y_down[1, j].wait_recv()
        forward_y(1, j)
    z_fwd_up[1].wait_recv()
    z_fwd_down[1].wait_recv()
    to_sibling((1, 2))
    y_fwd_up[0, 3].wait_recv()
    y_fwd_down[0, 3].wait_recv()
    x_over[2, 3] = send_piece((0, 2), (1, 2), 3, xn)
    attend([C], [2, 3])
    over[0, 2].wait_recv()
    over[1, 2].wait_recv()
    project(E)

    @pl.loop(0, 2)
    def _(i):
        attend([E], [2 * i, 2 * i + 1])

    attend([A, B, C, E], [OWN])
    x_over[1, 3].wait_recv()
    x_over[3, 3].wait_recv()

    @pl.loop(4, 6)
    def _(place):
        attend([A, B, C, E], [place])

    for j in range(3):
        y_fwd_up[0, j].wait_recv()
        y_fwd_down[0, j].wait_recv()
    for j in range(3):
        y_fwd_up[1, j].wait_recv()
        y_fwd_down[1, j].wait_recv()
    x_over[2, 3].wait_recv()
    loads["wo"].wait()
    loads["noise"].wait()

    for copy in started:
        copy.wait_send()
    started.clear()
    p0 = g.at[pl.ds(0, 8 * ROWS)]
    p1 = g.at[pl.ds(8 * ROWS, 8 * ROWS)]
    part_over = {}

    def rows_at(place, first=0, count=ROWS):
        return pl.ds(place * ROWS + first, count)

    def finish(group):
        attend([group], [6, 7])
        rows = pl.ds(group * GROUP, GROUP)
        for h in range(W // HD):
            lead = h * 2 * HD
            att[:, h * HD : (h + 1) * HD] = (
                acc[rows, lead : lead + HD] / acc[rows, lead + HD : lead + 2 * HD]
            ).astype(jnp.bfloat16)

        @pl.loop(0, 10)
        def _(i):
            cols = pl.ds(pl.multiple_of(i * 512, 512), 512)
            y = jnp.dot(att[...], wo[:, cols], preferred_element_type=jnp.float32)
            y = y.astype(jnp.bfloat16)
            p0[rows_at(2 * group), cols] = y[:ROWS]
            p1[rows_at(2 * group), cols] = y[ROWS : 2 * ROWS]
            p0[rows_at(2 * group + 1), cols] = y[2 * ROWS : 3 * ROWS]
            p1[rows_at(2 * group + 1), cols] = y[3 * ROWS :]

        for place in (2 * group + 1, 2 * group):
            part_over[place] = send(p1.at[rows_at(place)], s.at[place], sib)

    def total(dst, *terms):
        count = dst.shape[0] // 16

        @pl.loop(0, count)
        def _(i):
            rows = pl.ds(pl.multiple_of(i * 16, 16), 16)
            value = terms[0][rows, :].astype(jnp.float32)
            for term in terms[1:]:
                value = value + term[rows, :].astype(jnp.float32)
            dst[rows, :] = value.astype(jnp.bfloat16)

    a, b = pl.ds(0, HALF), pl.ds(HALF, HALF)
    quarter = HALF // 2
    x_first, hop_up, hop_down, end_up, end_down = {}, {}, {}, {}, {}

    def to_partner(z):
        place = PLACE[1, z]
        part_over[place].wait_recv()
        total(p0.at[rows_at(place, 0, HALF)], p0.at[rows_at(place, 0, HALF)], s.at[place, a])
        x_first[z] = send(p0.at[rows_at(place, 0, HALF)], xf.at[z], x2)

    def first_hop(way, place, rows, *terms):
        total(p0.at[rows_at(place, rows.start, rows.size)], p0.at[rows_at(place, rows.start, rows.size)], s.at[place, rows], *terms)
        hop_up[way] = send(p0.at[rows_at(place, rows.start, quarter)], r1.at[way, 0], zp)
        hop_down[way] = send(p0.at[rows_at(place, rows.start + quarter, quarter)], r1.at[way, 1], zm)

    def second_hop(way, up, down, rows, up_terms=(), down_terms=()):
        total(p0.at[rows_at(up, rows.start, rows.size)], p0.at[rows_at(up, rows.start, rows.size)], s.at[up, rows], *up_terms)
        total(p0.at[rows_at(down, rows.start, rows.size)], p0.at[rows_at(down, rows.start, rows.size)], s.at[down, rows], *down_terms)
        low, high = pl.ds(rows.start, quarter), pl.ds(rows.start + quarter, quarter)
        hop_up[way].wait_recv()
        total(p0.at[rows_at(up, low.start, quarter)], p0.at[rows_at(up, low.start, quarter)], r1.at[way, 0])
        end_up[way] = send(p0.at[rows_at(up, rows.start, rows.size)], r2.at[way, 0], zp)
        hop_down[way].wait_recv()
        total(p0.at[rows_at(down, high.start, quarter)], p0.at[rows_at(down, high.start, quarter)], r1.at[way, 1])
        end_down[way] = send(p0.at[rows_at(down, rows.start, rows.size)], r2.at[way, 1], zm)

    finish(E)
    finish(C)
    to_partner(2)
    first_hop(1, PLACE[1, 2], b)
    part_over[PLACE[0, 2]].wait_recv()
    first_hop(0, PLACE[0, 2], b)
    finish(B)
    to_partner(1)
    to_partner(3)
    second_hop(1, PLACE[1, 1], PLACE[1, 3], b)
    finish(A)
    to_partner(0)
    part_over[PLACE[0, 1]].wait_recv()
    part_over[PLACE[0, 3]].wait_recv()
    second_hop(0, PLACE[0, 1], PLACE[0, 3], b)
    x_first[2].wait_recv()
    first_hop(2, PLACE[0, 2], a, xf.at[2])
    end_up[1].wait_recv()
    end_down[1].wait_recv()
    total(p0.at[rows_at(1, HALF, HALF)], p0.at[rows_at(1, HALF, HALF)], s.at[1, b], r2.at[1, 0], r2.at[1, 1])
    last = send(p0.at[rows_at(1, HALF, HALF)], xb, x2)
    x_first[1].wait_recv()
    x_first[3].wait_recv()
    second_hop(2, PLACE[0, 1], PLACE[0, 3], a, (xf.at[1],), (xf.at[3],))
    part_over[0].wait_recv()

    def renoise(way, first, partner):
        @pl.loop(0, HALF // 16)
        def _(i):
            rows = pl.ds(pl.multiple_of(first + i * 16, 16), 16)
            here = pl.ds(pl.multiple_of(i * 16, 16), 16)
            mixed = p0[rows, :].astype(jnp.float32) + s[0, rows, :].astype(jnp.float32)
            mixed = mixed + r2[way, 0, here, :].astype(jnp.float32) + r2[way, 1, here, :].astype(jnp.float32)
            mixed = mixed + partner[here, :].astype(jnp.float32)
            xrows = lat[rows, :].astype(jnp.float32)
            fresh = noise[rows, :].astype(jnp.float32)
            result = (1.0 - level_next) * (xrows - level_now * (xrows + mixed)) + level_next * fresh
            out[0, rows, :] = result.astype(jnp.bfloat16)

    end_up[0].wait_recv()
    end_down[0].wait_recv()
    last.wait_recv()
    renoise(0, HALF, xb)
    x_first[0].wait_recv()
    end_up[2].wait_recv()
    end_down[2].wait_recv()
    renoise(2, 0, xf.at[0])

    for copy in started:
        copy.wait_send()


def local(*operands):
    operands = operands[:9] + (operands[9].T,) + operands[10:]
    bf16, f32 = jnp.bfloat16, jnp.float32
    anywhere = pl.BlockSpec(memory_space=pl.ANY)
    vmem = pl.BlockSpec(memory_space=pltpu.VMEM)
    smem = pl.BlockSpec(memory_space=pltpu.SMEM)
    return pl.pallas_call(
        kernel,
        out_shape=jax.ShapeDtypeStruct((1, ROWS, D), bf16),
        in_specs=[anywhere] * 8 + [vmem] + [smem] * 4,
        out_specs=vmem,
        scratch_shapes=[
            pltpu.VMEM((ROWS, D), bf16),
            pltpu.VMEM((ROWS, D), bf16),
            pltpu.VMEM((3, D, W), bf16),
            pltpu.VMEM((W, D), bf16),
            pltpu.VMEM((TOK, D), bf16),
            pltpu.VMEM((9, 2, TOK, W), bf16),
            pltpu.VMEM((TOK, W), bf16),
            pltpu.VMEM((TOK, 2 * W), f32),
            pltpu.VMEM((TOK, W), f32),
            pltpu.VMEM((GROUP, W), bf16),
            pltpu.VMEM((8, ROWS, D), bf16),
            pltpu.VMEM((3, 2, HALF // 2, D), bf16),
            pltpu.VMEM((3, 2, HALF, D), bf16),
            pltpu.VMEM((4, HALF, D), bf16),
            pltpu.VMEM((HALF, D), bf16),
            pltpu.SMEM((16,), jnp.int32),
            pltpu.SemaphoreType.DMA((8,)),
            pltpu.SemaphoreType.DMA((N_SEM,)),
            pltpu.SemaphoreType.DMA((N_SEM,)),
        ],
        compiler_params=pltpu.CompilerParams(
            collective_id=0, has_side_effects=True, vmem_limit_bytes=62 * 2**20
        ),
    )(*operands)


def solution(mesh):
    in_specs = (
        P("span", "seq", None),
        P("span", "seq", None),
        P("span", None, "seq"),
        P("span", None, "seq"),
        P(None, "seq"),
        P(None, "seq"),
        P(None, "seq"),
        P("seq", None),
        P(),
        P(),
        P(),
        P(),
        P(),
    )
    out_specs = P("span", "seq", None)
    return jax.shard_map(local, mesh=mesh, in_specs=in_specs, out_specs=out_specs, check_vma=False)
```

```python
import itertools

import jax
import jax.numpy as jnp
from jax import lax
from jax.experimental import pallas as pl
from jax.experimental.pallas import tpu as pltpu
from jax.sharding import PartitionSpec as P

HD = 128
D = 5120
TOK = 1024
W = 256
ROWS = 64
HALF = 32
GROUP = 256
PIECES = ((0, 240), (240, 240), (480, 224), (704, 320))
X_COLS = 2304
LOG2E = 1.4426950408889634
SCALE = LOG2E / HD**0.5
LOW = -1e30
HIGH = 3e38
MESH = pl.DeviceIdType.MESH
N_SEM = 144

PLACE = {(0, 0): 0, (1, 0): 1, (0, 1): 2, (0, 3): 3, (1, 1): 4, (1, 3): 5, (0, 2): 6, (1, 2): 7}
CACHE = {(0, 0): 0, (0, 1): 1, (0, 3): 2, (1, 0): 3, (1, 1): 4, (1, 3): 5, (0, 2): 6, (1, 2): 7}
OWN = 8
A, B, C, E = (0, 256), (256, 256), (512, 256), (768, 256)
E_LEFT, E_RIGHT = (768, 128), (896, 128)


def kernel(
    latent_hbm,
    noise_hbm,
    ck_hbm,
    cv_hbm,
    wq_hbm,
    wk_hbm,
    wv_hbm,
    wo_hbm,
    modulation,
    plan,
    step_index,
    assignment,
    visible,
    out,
    lat,
    noise,
    w,
    wo,
    g,
    kv,
    q,
    acc,
    top,
    att,
    s,
    r1_a,
    r1_b,
    r2_a,
    r2_b,
    xf,
    xb,
    flags,
    local_sem,
    send_sem,
    recv_sem,
):
    span = lax.axis_index("span")
    seq = lax.axis_index("seq")
    x_lo = span // 4
    y = span % 4
    x_hi = seq // 8
    z = (seq // 2) % 4
    core = seq % 2

    def seq_of(a, b, c):
        return a * 8 + b * 2 + c

    sib = (span, seq_of(x_hi, z, 1 - core))
    x2 = (span, seq_of(1 - x_hi, z, core))
    zp = (span, seq_of(x_hi, (z + 1) % 4, core))
    zm = (span, seq_of(x_hi, (z + 3) % 4, core))
    xn = ((1 - x_lo) * 4 + y, seq)
    yp = (x_lo * 4 + (y + 1) % 4, seq)
    ym = (x_lo * 4 + (y + 3) % 4, seq)

    loads = {}
    for i, (name, src, dst) in enumerate(
        (
            ("k", ck_hbm.at[0], kv.at[0, 0]),
            ("v", cv_hbm.at[0], kv.at[0, 1]),
            ("lat", latent_hbm.at[0], lat),
            ("wq", wq_hbm, w.at[0]),
            ("wk", wk_hbm, w.at[1]),
            ("wv", wv_hbm, w.at[2]),
            ("wo", wo_hbm, wo),
            ("noise", noise_hbm.at[0], noise),
        )
    ):
        loads[name] = pltpu.make_async_copy(src, dst, local_sem.at[i])
        loads[name].start()

    barrier = pltpu.get_barrier_semaphore()
    for device in (sib, x2, zp, zm, xn, yp, ym):
        pl.semaphore_signal(barrier, 1, device_id=device, device_id_type=MESH)
    started = []
    count = itertools.count()

    def send(src, dst, device):
        i = next(count)
        copy = pltpu.make_async_remote_copy(
            src, dst, send_sem.at[i], recv_sem.at[i], device_id=device, device_id_type=MESH
        )
        copy.start()
        started.append(copy)
        return copy

    def piece(place, j):
        return kv.at[place, :, pl.ds(*PIECES[j])]

    def part(place, side, j):
        return kv.at[place, side, pl.ds(*PIECES[j])]

    def send_piece(src, dst, j, device):
        return send(piece(CACHE[src], j), piece(CACHE[dst], j), device)

    def rows_of(place, sub, half=None):
        base = PLACE[place] * 2 * ROWS + sub * ROWS
        if half is None:
            return g.at[pl.ds(base, ROWS)]
        return g.at[pl.ds(base + half * HALF, HALF)]

    step = step_index[span]
    level_now = plan[0, step]
    level_next = plan[1, step]
    loads["lat"].wait()

    @pl.loop(0, 4)
    def _(i):
        rows = pl.ds(pl.multiple_of(i * 16, 16), 16)
        values = lat[rows, :].astype(jnp.float32)
        rms = lax.rsqrt(jnp.mean(values * values, axis=1, keepdims=True) + 1e-06)
        shift = modulation[step, 0:1, :]
        scale = modulation[step, 1:2, :]
        g[rows, :] = (values * rms * (1.0 + scale) + shift).astype(jnp.bfloat16)

    mine = assignment[span]
    for (dx, dy), place in CACHE.items():
        other = ((x_lo + dx) % 2) * 4 + (y + dy) % 4
        flags[place] = visible[mine, assignment[other]]
    flags[OWN] = 1

    acc[...] = jnp.zeros_like(acc)
    top[...] = jnp.full_like(top, LOW)

    pl.semaphore_wait(barrier, 7)
    x_part, z_up, z_down, over = {}, {}, {}, {}
    for h in range(2):
        x_part[h] = send(rows_of((0, 0), 0, h), rows_of((1, 0), 0, h), x2)
    for h in range(2):
        z_up[0, h] = send(rows_of((0, 0), 0, h), rows_of((0, 3), 0, h), zp)
        z_down[0, h] = send(rows_of((0, 0), 0, h), rows_of((0, 1), 0, h), zm)

    def to_sibling(place):
        over[place] = send(rows_of(place, 0), rows_of(place, 1), sib)

    to_sibling((0, 0))

    loads["k"].wait()
    loads["v"].wait()
    y_up, y_down, x_over = {}, {}, {}
    for j in range(4):
        y_up[0, j] = send_piece((0, 0), (0, 3), j, yp)
        y_down[0, j] = send_piece((0, 0), (0, 1), j, ym)
    for j in range(3):
        x_over[0, j] = send_piece((0, 0), (1, 0), j, xn)

    for h in range(2):
        x_part[h].wait_recv()
        z_up[1, h] = send(rows_of((1, 0), 0, h), rows_of((1, 3), 0, h), zp)
        z_down[1, h] = send(rows_of((1, 0), 0, h), rows_of((1, 1), 0, h), zm)
    to_sibling((1, 0))
    def project(group):
        rows = pl.ds(*group)

        @pl.loop(0, 3)
        def _(i):
            y = jnp.dot(g[rows, :], w[i], preferred_element_type=jnp.float32)
            y = (y * jnp.where(i == 0, SCALE, 1.0)).astype(jnp.bfloat16)

            @pl.when(i == 0)
            def _():
                q[rows, :] = y

            @pl.when(i > 0)
            def _():
                kv[OWN, i - 1, rows, :] = y

    ones = jnp.ones((TOK, HD), jnp.bfloat16)

    def attend(groups, places):
        items = [(pl.ds(*group), h) for group in groups for h in range(W // HD)]
        seen = [jnp.full((8, HD), flags[place], jnp.int32) > 0 for place in places]
        seen = [{count: jnp.tile(mark, (count // 8, 1)) for _, count in groups} for mark in seen]
        olds = [top[rows, h * HD : (h + 1) * HD] for rows, h in items]
        scores, results = {}, {}

        def score(i):
            rows, h = items[i]
            cols = slice(h * HD, (h + 1) * HD)
            scores[i] = [
                lax.dot_general(
                    q[rows, cols],
                    kv[place, 0, :, cols],
                    (((1,), (1,)), ((), ())),
                    preferred_element_type=jnp.float32,
                )
                for place in places
            ]

        def weigh(i):
            rows, h = items[i]
            cols = slice(h * HD, (h + 1) * HD)
            new = olds[i]
            marks = [mark[rows.size] for mark in seen]
            for mark, block in zip(marks, scores[i]):
                new = jnp.where(mark, jnp.maximum(new, jnp.max(block, axis=1, keepdims=True)), new)
            shrink = jnp.exp2(olds[i] - new)
            lead = h * 2 * HD
            value = acc[rows, lead : lead + HD] * shrink
            total = acc[rows, lead + HD : lead + 2 * HD] * shrink
            for mark, block, place in zip(marks, scores[i], places):
                low = jnp.where(mark, new, HIGH)
                weights = jnp.exp2(block - jnp.tile(low, (1, TOK // HD))).astype(jnp.bfloat16)
                both = jnp.concatenate((kv[place, 1, :, cols], ones), axis=1)
                sums = jnp.dot(weights, both, preferred_element_type=jnp.float32)
                value = value + sums[:, :HD]
                total = total + sums[:, HD:]
            results[i] = (new, value, total)

        score(0)
        for i in range(len(items)):
            if i + 1 < len(items):
                score(i + 1)
            weigh(i)
        for i, (rows, h) in enumerate(items):
            lead = h * 2 * HD
            top[rows, h * HD : (h + 1) * HD], acc[rows, lead : lead + HD], acc[rows, lead + HD : lead + 2 * HD] = (
                results[i]
            )

    z_fwd_up, z_fwd_down = {}, {}

    def forward_z(x):
        for h in range(2):
            z_up[x, h].wait_recv()
            z_down[x, h].wait_recv()
        z_fwd_up[x] = send(rows_of((x, 3), 0, 0), rows_of((x, 2), 0, 0), zp)
        z_fwd_down[x] = send(rows_of((x, 1), 0, 1), rows_of((x, 2), 0, 1), zm)
        to_sibling((x, 3))
        to_sibling((x, 1))

    y_fwd_up, y_fwd_down = {}, {}

    def forward_y(x, j):
        y_fwd_up[x, j] = send(part(CACHE[x, 3], 0, j), part(CACHE[x, 2], 0, j), yp)
        y_fwd_down[x, j] = send(part(CACHE[x, 1], 1, j), part(CACHE[x, 2], 1, j), ym)

    def forward_x(j):
        x_over[0, j].wait_recv()
        y_up[1, j] = send_piece((1, 0), (1, 3), j, yp)
        y_down[1, j] = send_piece((1, 0), (1, 1), j, ym)

    forward_z(0)
    for name in ("wq", "wk", "wv"):
        loads[name].wait()
    over[0, 0].wait_recv()
    over[1, 0].wait_recv()
    project(A)
    forward_x(0)
    over[0, 1].wait_recv()
    over[0, 3].wait_recv()
    project(B)
    attend([A, B], [0])
    for j in range(4):
        y_up[0, j].wait_recv()
        y_down[0, j].wait_recv()
    forward_x(1)
    for dy in (0, 1, 3):
        x_over[dy, 3] = send_piece((0, dy), (1, dy), 3, xn)

    @pl.loop(1, 3)
    def _(place):
        attend([A, B], [place])

    forward_x(2)
    for j in (3, 0, 1, 2):
        forward_y(0, j)
    forward_z(1)
    over[1, 1].wait_recv()
    over[1, 3].wait_recv()
    project(C)
    attend([C], [0, 1])
    z_fwd_up[0].wait_recv()
    z_fwd_down[0].wait_recv()
    to_sibling((0, 2))
    x_over[0, 3].wait_recv()
    attend([A, B], [3])
    attend([C], [2, 3])
    over[0, 2].wait_recv()
    project(E_LEFT)
    for j in range(3):
        y_up[1, j].wait_recv()
        y_down[1, j].wait_recv()
        forward_y(1, j)
    y_fwd_up[0, 3].wait_recv()
    y_fwd_down[0, 3].wait_recv()
    x_over[2, 3] = send_piece((0, 2), (1, 2), 3, xn)
    z_fwd_up[1].wait_recv()
    z_fwd_down[1].wait_recv()
    to_sibling((1, 2))
    attend([E_LEFT], [0, 1, 2, 3])
    x_over[1, 3].wait_recv()
    attend([A, B, C, E_LEFT], [4])
    over[1, 2].wait_recv()
    project(E_RIGHT)
    attend([E_RIGHT], [0, 1, 2, 3, 4])
    attend([A, B, C, E], [OWN])
    x_over[3, 3].wait_recv()
    for j in range(3):
        y_fwd_up[0, j].wait_recv()
        y_fwd_down[0, j].wait_recv()

    @pl.loop(5, 7)
    def _(place):
        attend([A, B, C, E], [place])

    for j in range(3):
        y_fwd_up[1, j].wait_recv()
        y_fwd_down[1, j].wait_recv()
    x_over[2, 3].wait_recv()
    loads["wo"].wait()
    loads["noise"].wait()

    for copy in started:
        copy.wait_send()
    started.clear()
    p0 = g.at[pl.ds(0, 8 * ROWS)]
    p1 = g.at[pl.ds(8 * ROWS, 8 * ROWS)]
    part_over = {}

    def rows_at(place, first=0, count=ROWS):
        return pl.ds(place * ROWS + first, count)

    def finish(group):
        attend([group], [7])
        rows = pl.ds(*group)
        for h in range(W // HD):
            lead = h * 2 * HD
            att[:, h * HD : (h + 1) * HD] = (
                acc[rows, lead : lead + HD] / acc[rows, lead + HD : lead + 2 * HD]
            ).astype(jnp.bfloat16)
        first = group[0] // (2 * ROWS)

        @pl.loop(0, 2)
        def _(i):
            for k in range(5):
                cols = pl.ds(pl.multiple_of(i * (D // 2) + k * 512, 512), 512)
                y = jnp.dot(att[...], wo[:, cols], preferred_element_type=jnp.float32)
                y = y.astype(jnp.bfloat16)
                p0[rows_at(first), cols] = y[:ROWS]
                p1[rows_at(first), cols] = y[ROWS : 2 * ROWS]
                p0[rows_at(first + 1), cols] = y[2 * ROWS : 3 * ROWS]
                p1[rows_at(first + 1), cols] = y[3 * ROWS :]

        for place in (first + 1, first):
            part_over[place] = send(p1.at[rows_at(place)], s.at[place], sib)

    def total(dst, *terms):
        count = dst.shape[0] // 16

        @pl.loop(0, count)
        def _(i):
            rows = pl.ds(pl.multiple_of(i * 16, 16), 16)
            value = terms[0][rows, :].astype(jnp.float32)
            for term in terms[1:]:
                value = value + term[rows, :].astype(jnp.float32)
            dst[rows, :] = value.astype(jnp.bfloat16)

    a, b = pl.ds(0, X_COLS), pl.ds(X_COLS, D - X_COLS)
    x_first, hop_up, hop_down, end_up, end_down = {}, {}, {}, {}, {}

    def sum_at(place, cols, *terms, first=0, count=ROWS):
        dst = p0.at[rows_at(place, first, count), cols]
        total(dst, dst, *terms)

    def to_partner(z):
        place = PLACE[1, z]
        part_over[place].wait_recv()
        sum_at(place, a, s.at[place, :, a])
        x_first[z] = send(p0.at[rows_at(place), a], xf.at[z], x2)

    def first_hop(way, place, cols, r1, *terms):
        sum_at(place, cols, s.at[place, :, cols], *terms)
        hop_up[way] = send(p0.at[rows_at(place, 0, HALF), cols], r1.at[0], zp)
        hop_down[way] = send(p0.at[rows_at(place, HALF, HALF), cols], r1.at[1], zm)

    def second_hop(way, up, down, cols, r1, r2, up_terms=(), down_terms=()):
        sum_at(up, cols, s.at[up, :, cols], *up_terms)
        sum_at(down, cols, s.at[down, :, cols], *down_terms)
        hop_up[way].wait_recv()
        sum_at(up, cols, r1.at[0], count=HALF)
        end_up[way] = send(p0.at[rows_at(up), cols], r2.at[0], zp)
        hop_down[way].wait_recv()
        sum_at(down, cols, r1.at[1], first=HALF, count=HALF)
        end_down[way] = send(p0.at[rows_at(down), cols], r2.at[1], zm)

    finish(E)
    finish(C)
    to_partner(2)
    first_hop(1, PLACE[1, 2], b, r1_b.at[1])
    part_over[PLACE[0, 2]].wait_recv()
    first_hop(0, PLACE[0, 2], b, r1_b.at[0])
    finish(B)
    to_partner(1)
    to_partner(3)
    second_hop(1, PLACE[1, 1], PLACE[1, 3], b, r1_b.at[1], r2_b.at[1])
    finish(A)
    to_partner(0)
    part_over[PLACE[0, 1]].wait_recv()
    part_over[PLACE[0, 3]].wait_recv()
    second_hop(0, PLACE[0, 1], PLACE[0, 3], b, r1_b.at[0], r2_b.at[0])
    x_first[2].wait_recv()
    first_hop(2, PLACE[0, 2], a, r1_a, xf.at[2])
    end_up[1].wait_recv()
    end_down[1].wait_recv()
    sum_at(1, b, s.at[1, :, b], r2_b.at[1, 0], r2_b.at[1, 1])
    last = send(p0.at[rows_at(1), b], xb, x2)
    x_first[1].wait_recv()
    x_first[3].wait_recv()
    second_hop(2, PLACE[0, 1], PLACE[0, 3], a, r1_a, r2_a, (xf.at[1],), (xf.at[3],))
    part_over[0].wait_recv()

    def renoise(cols, r2, partner):
        @pl.loop(0, ROWS // 16)
        def _(i):
            rows = pl.ds(pl.multiple_of(i * 16, 16), 16)
            mixed = p0[rows, cols].astype(jnp.float32) + s[0, rows, cols].astype(jnp.float32)
            mixed = mixed + r2[0, rows, :].astype(jnp.float32) + r2[1, rows, :].astype(jnp.float32)
            mixed = mixed + partner[rows, :].astype(jnp.float32)
            xrows = lat[rows, cols].astype(jnp.float32)
            fresh = noise[rows, cols].astype(jnp.float32)
            result = (1.0 - level_next) * (xrows - level_now * (xrows + mixed)) + level_next * fresh
            out[0, rows, cols] = result.astype(jnp.bfloat16)

    end_up[0].wait_recv()
    end_down[0].wait_recv()
    last.wait_recv()
    renoise(b, r2_b.at[0], xb)
    x_first[0].wait_recv()
    end_up[2].wait_recv()
    end_down[2].wait_recv()
    renoise(a, r2_a, xf.at[0])

    for copy in started:
        copy.wait_send()


def local(*operands):
    operands = operands[:9] + (operands[9].T,) + operands[10:]
    bf16, f32 = jnp.bfloat16, jnp.float32
    anywhere = pl.BlockSpec(memory_space=pl.ANY)
    vmem = pl.BlockSpec(memory_space=pltpu.VMEM)
    smem = pl.BlockSpec(memory_space=pltpu.SMEM)
    return pl.pallas_call(
        kernel,
        out_shape=jax.ShapeDtypeStruct((1, ROWS, D), bf16),
        in_specs=[anywhere] * 8 + [vmem] + [smem] * 4,
        out_specs=vmem,
        scratch_shapes=[
            pltpu.VMEM((ROWS, D), bf16),
            pltpu.VMEM((ROWS, D), bf16),
            pltpu.VMEM((3, D, W), bf16),
            pltpu.VMEM((W, D), bf16),
            pltpu.VMEM((TOK, D), bf16),
            pltpu.VMEM((9, 2, TOK, W), bf16),
            pltpu.VMEM((TOK, W), bf16),
            pltpu.VMEM((TOK, 2 * W), f32),
            pltpu.VMEM((TOK, W), f32),
            pltpu.VMEM((GROUP, W), bf16),
            pltpu.VMEM((8, ROWS, D), bf16),
            pltpu.VMEM((2, HALF, X_COLS), bf16),
            pltpu.VMEM((2, 2, HALF, D - X_COLS), bf16),
            pltpu.VMEM((2, ROWS, X_COLS), bf16),
            pltpu.VMEM((2, 2, ROWS, D - X_COLS), bf16),
            pltpu.VMEM((4, ROWS, X_COLS), bf16),
            pltpu.VMEM((ROWS, D - X_COLS), bf16),
            pltpu.SMEM((16,), jnp.int32),
            pltpu.SemaphoreType.DMA((8,)),
            pltpu.SemaphoreType.DMA((N_SEM,)),
            pltpu.SemaphoreType.DMA((N_SEM,)),
        ],
        compiler_params=pltpu.CompilerParams(
            collective_id=0, has_side_effects=True, vmem_limit_bytes=62 * 2**20
        ),
    )(*operands)


def solution(mesh):
    in_specs = (
        P("span", "seq", None),
        P("span", "seq", None),
        P("span", None, "seq"),
        P("span", None, "seq"),
        P(None, "seq"),
        P(None, "seq"),
        P(None, "seq"),
        P("seq", None),
        P(),
        P(),
        P(),
        P(),
        P(),
    )
    out_specs = P("span", "seq", None)
    return jax.shard_map(local, mesh=mesh, in_specs=in_specs, out_specs=out_specs, check_vma=False)
```

```python
import itertools

import jax
import jax.numpy as jnp
from jax import lax
from jax.experimental import pallas as pl
from jax.experimental.pallas import tpu as pltpu
from jax.sharding import PartitionSpec as P

HD = 128
D = 5120
TOK = 1024
W = 256
ROWS = 64
HALF = 32
PIECES = ((0, 240), (240, 240), (480, 224), (704, 320))
X_COLS = 2304
LOG2E = 1.4426950408889634
SCALE = LOG2E / HD**0.5
LOW = -1e30
HIGH = 3e38
MESH = pl.DeviceIdType.MESH
N_SEM = 144

PLACE = {(0, 0): 0, (1, 0): 1, (0, 1): 2, (0, 3): 3, (1, 1): 4, (1, 3): 5, (0, 2): 6, (1, 2): 7}
CACHE = {(0, 0): 0, (0, 1): 1, (0, 3): 2, (1, 0): 3, (1, 1): 4, (1, 3): 5, (0, 2): 6, (1, 2): 7}
OWN = 8
A, B, C, E = (0, 256), (256, 256), (512, 256), (768, 256)
E_LEFT, E_RIGHT = (768, 128), (896, 128)


def kernel(
    latent_hbm,
    noise_hbm,
    ck_hbm,
    cv_hbm,
    wq_hbm,
    wk_hbm,
    wv_hbm,
    wo_hbm,
    modulation,
    plan,
    step_index,
    assignment,
    visible,
    out,
    lat,
    noise,
    w,
    wo,
    g,
    kv,
    q,
    acc,
    top,
    att,
    s,
    r1_a,
    r1_b,
    r2_a,
    r2_b,
    xf,
    xb,
    flags,
    local_sem,
    send_sem,
    recv_sem,
):
    span = lax.axis_index("span")
    seq = lax.axis_index("seq")
    x_lo = span // 4
    y = span % 4
    x_hi = seq // 8
    z = (seq // 2) % 4
    core = seq % 2

    def seq_of(a, b, c):
        return a * 8 + b * 2 + c

    sib = (span, seq_of(x_hi, z, 1 - core))
    x2 = (span, seq_of(1 - x_hi, z, core))
    zp = (span, seq_of(x_hi, (z + 1) % 4, core))
    zm = (span, seq_of(x_hi, (z + 3) % 4, core))
    xn = ((1 - x_lo) * 4 + y, seq)
    yp = (x_lo * 4 + (y + 1) % 4, seq)
    ym = (x_lo * 4 + (y + 3) % 4, seq)

    loads = {}
    for i, (name, src, dst) in enumerate(
        (
            ("k", ck_hbm.at[0], kv.at[0, 0]),
            ("v", cv_hbm.at[0], kv.at[0, 1]),
            ("lat", latent_hbm.at[0], lat),
            ("wq", wq_hbm, w.at[0]),
            ("wk", wk_hbm, w.at[1]),
            ("wv", wv_hbm, w.at[2]),
            ("wo", wo_hbm, wo),
            ("noise", noise_hbm.at[0], noise),
        )
    ):
        loads[name] = pltpu.make_async_copy(src, dst, local_sem.at[i])
        loads[name].start()

    barrier = pltpu.get_barrier_semaphore()
    for device in (sib, x2, zp, zm, xn, yp, ym):
        pl.semaphore_signal(barrier, 1, device_id=device, device_id_type=MESH)
    started = []
    count = itertools.count()

    def send(src, dst, device):
        i = next(count)
        copy = pltpu.make_async_remote_copy(
            src, dst, send_sem.at[i], recv_sem.at[i], device_id=device, device_id_type=MESH
        )
        copy.start()
        started.append(copy)
        return copy

    def piece(place, j):
        return kv.at[place, :, pl.ds(*PIECES[j])]

    def part(place, side, j):
        return kv.at[place, side, pl.ds(*PIECES[j])]

    def send_piece(src, dst, j, device):
        return send(piece(CACHE[src], j), piece(CACHE[dst], j), device)

    def rows_of(place, sub, half=None):
        base = PLACE[place] * 2 * ROWS + sub * ROWS
        if half is None:
            return g.at[pl.ds(base, ROWS)]
        return g.at[pl.ds(base + half * HALF, HALF)]

    step = step_index[span]
    level_now = plan[0, step]
    level_next = plan[1, step]
    loads["lat"].wait()

    @pl.loop(0, 4)
    def _(i):
        rows = pl.ds(pl.multiple_of(i * 16, 16), 16)
        values = lat[rows, :].astype(jnp.float32)
        rms = lax.rsqrt(jnp.mean(values * values, axis=1, keepdims=True) + 1e-06)
        shift = modulation[step, 0:1, :]
        scale = modulation[step, 1:2, :]
        g[rows, :] = (values * rms * (1.0 + scale) + shift).astype(jnp.bfloat16)

    mine = assignment[span]
    for (dx, dy), place in CACHE.items():
        other = ((x_lo + dx) % 2) * 4 + (y + dy) % 4
        flags[place] = visible[mine, assignment[other]]
    flags[OWN] = 1

    acc[...] = jnp.zeros_like(acc)
    top[...] = jnp.full_like(top, LOW)

    pl.semaphore_wait(barrier, 7)
    x_part, z_up, z_down, over = {}, {}, {}, {}
    for h in range(2):
        x_part[h] = send(rows_of((0, 0), 0, h), rows_of((1, 0), 0, h), x2)
    for h in range(2):
        z_up[0, h] = send(rows_of((0, 0), 0, h), rows_of((0, 3), 0, h), zp)
        z_down[0, h] = send(rows_of((0, 0), 0, h), rows_of((0, 1), 0, h), zm)

    def to_sibling(place):
        over[place] = send(rows_of(place, 0), rows_of(place, 1), sib)

    to_sibling((0, 0))

    loads["k"].wait()
    loads["v"].wait()
    y_up, y_down, x_over = {}, {}, {}
    for j in range(4):
        y_up[0, j] = send_piece((0, 0), (0, 3), j, yp)
        y_down[0, j] = send_piece((0, 0), (0, 1), j, ym)
    for j in range(3):
        x_over[0, j] = send_piece((0, 0), (1, 0), j, xn)

    for h in range(2):
        x_part[h].wait_recv()
        z_up[1, h] = send(rows_of((1, 0), 0, h), rows_of((1, 3), 0, h), zp)
        z_down[1, h] = send(rows_of((1, 0), 0, h), rows_of((1, 1), 0, h), zm)
    to_sibling((1, 0))
    def project(group):
        rows = pl.ds(*group)

        @pl.loop(0, 3)
        def _(i):
            y = jnp.dot(g[rows, :], w[i], preferred_element_type=jnp.float32)
            y = (y * jnp.where(i == 0, SCALE, 1.0)).astype(jnp.bfloat16)

            @pl.when(i == 0)
            def _():
                q[rows, :] = y

            @pl.when(i > 0)
            def _():
                kv[OWN, i - 1, rows, :] = y

    ones = jnp.ones((TOK, HD), jnp.bfloat16)

    def attend(groups, places):
        items = [(pl.ds(*group), h) for group in groups for h in range(W // HD)]
        seen = [jnp.full((8, HD), flags[place], jnp.int32) > 0 for place in places]
        seen = [{count: jnp.tile(mark, (count // 8, 1)) for _, count in groups} for mark in seen]
        olds = [top[rows, h * HD : (h + 1) * HD] for rows, h in items]
        scores, results = {}, {}

        def score(i):
            rows, h = items[i]
            cols = slice(h * HD, (h + 1) * HD)
            scores[i] = [
                lax.dot_general(
                    q[rows, cols],
                    kv[place, 0, :, cols],
                    (((1,), (1,)), ((), ())),
                    preferred_element_type=jnp.float32,
                )
                for place in places
            ]

        def weigh(i):
            rows, h = items[i]
            cols = slice(h * HD, (h + 1) * HD)
            new = olds[i]
            marks = [mark[rows.size] for mark in seen]
            for mark, block in zip(marks, scores[i]):
                new = jnp.where(mark, jnp.maximum(new, jnp.max(block, axis=1, keepdims=True)), new)
            shrink = jnp.exp2(olds[i] - new)
            lead = h * 2 * HD
            value = acc[rows, lead : lead + HD] * shrink
            total = acc[rows, lead + HD : lead + 2 * HD] * shrink
            for mark, block, place in zip(marks, scores[i], places):
                low = jnp.where(mark, new, HIGH)
                weights = jnp.exp2(block - jnp.tile(low, (1, TOK // HD))).astype(jnp.bfloat16)
                both = jnp.concatenate((kv[place, 1, :, cols], ones), axis=1)
                sums = jnp.dot(weights, both, preferred_element_type=jnp.float32)
                value = value + sums[:, :HD]
                total = total + sums[:, HD:]
            results[i] = (new, value, total)

        score(0)
        for i in range(len(items)):
            if i + 1 < len(items):
                score(i + 1)
            weigh(i)
        for i, (rows, h) in enumerate(items):
            lead = h * 2 * HD
            top[rows, h * HD : (h + 1) * HD], acc[rows, lead : lead + HD], acc[rows, lead + HD : lead + 2 * HD] = (
                results[i]
            )

    z_fwd_up, z_fwd_down = {}, {}

    def forward_z(x):
        for h in range(2):
            z_up[x, h].wait_recv()
            z_down[x, h].wait_recv()
        z_fwd_up[x] = send(rows_of((x, 3), 0, 0), rows_of((x, 2), 0, 0), zp)
        z_fwd_down[x] = send(rows_of((x, 1), 0, 1), rows_of((x, 2), 0, 1), zm)
        to_sibling((x, 3))
        to_sibling((x, 1))

    y_fwd_up, y_fwd_down = {}, {}

    def forward_y(x, j):
        y_fwd_up[x, j] = send(part(CACHE[x, 3], 0, j), part(CACHE[x, 2], 0, j), yp)
        y_fwd_down[x, j] = send(part(CACHE[x, 1], 1, j), part(CACHE[x, 2], 1, j), ym)

    def forward_x(j):
        x_over[0, j].wait_recv()
        y_up[1, j] = send_piece((1, 0), (1, 3), j, yp)
        y_down[1, j] = send_piece((1, 0), (1, 1), j, ym)

    forward_z(0)
    for name in ("wq", "wk", "wv"):
        loads[name].wait()
    over[0, 0].wait_recv()
    over[1, 0].wait_recv()
    project(A)
    forward_x(0)
    over[0, 1].wait_recv()
    over[0, 3].wait_recv()
    project(B)
    attend([A, B], [0])
    for j in range(4):
        y_up[0, j].wait_recv()
        y_down[0, j].wait_recv()
    forward_x(1)
    for dy in (0, 1, 3):
        x_over[dy, 3] = send_piece((0, dy), (1, dy), 3, xn)

    @pl.loop(1, 3)
    def _(place):
        attend([A, B], [place])

    forward_x(2)
    for j in (3, 0, 1, 2):
        forward_y(0, j)
    forward_z(1)
    over[1, 1].wait_recv()
    over[1, 3].wait_recv()
    project(C)
    attend([C], [0, 1])
    z_fwd_up[0].wait_recv()
    z_fwd_down[0].wait_recv()
    to_sibling((0, 2))
    x_over[0, 3].wait_recv()
    attend([A, B], [3])
    attend([C], [2, 3])
    over[0, 2].wait_recv()
    project(E_LEFT)
    for j in range(3):
        y_up[1, j].wait_recv()
        y_down[1, j].wait_recv()
        forward_y(1, j)
    y_fwd_up[0, 3].wait_recv()
    y_fwd_down[0, 3].wait_recv()
    x_over[2, 3] = send_piece((0, 2), (1, 2), 3, xn)
    z_fwd_up[1].wait_recv()
    z_fwd_down[1].wait_recv()
    to_sibling((1, 2))
    attend([E_LEFT], [0, 1, 2, 3])
    x_over[1, 3].wait_recv()
    attend([A, B, C, E_LEFT], [4])
    over[1, 2].wait_recv()
    project(E_RIGHT)
    attend([E_RIGHT], [0, 1, 2, 3, 4])
    attend([A, B, C, E], [OWN])
    x_over[3, 3].wait_recv()
    for j in range(3):
        y_fwd_up[0, j].wait_recv()
        y_fwd_down[0, j].wait_recv()

    attend([E], [5, 6])
    for j in range(3):
        y_fwd_up[1, j].wait_recv()
        y_fwd_down[1, j].wait_recv()
    x_over[2, 3].wait_recv()
    loads["wo"].wait()
    loads["noise"].wait()

    for copy in started:
        copy.wait_send()
    started.clear()
    p0 = g.at[pl.ds(0, 8 * ROWS)]
    p1 = g.at[pl.ds(8 * ROWS, 8 * ROWS)]
    part_over = {}

    def rows_at(place, first=0, count=ROWS):
        return pl.ds(place * ROWS + first, count)

    def finish(group, places):
        attend([group], places)
        start, count = group
        rows, here = pl.ds(start, count), pl.ds(0, count)
        for h in range(W // HD):
            lead = h * 2 * HD
            att[here, h * HD : (h + 1) * HD] = (
                acc[rows, lead : lead + HD] / acc[rows, lead + HD : lead + 2 * HD]
            ).astype(jnp.bfloat16)
        blocks = range(start // (2 * ROWS), (start + count) // (2 * ROWS))

        @pl.loop(0, 2)
        def _(i):
            for k in range(5):
                cols = pl.ds(pl.multiple_of(i * (D // 2) + k * 512, 512), 512)
                y = jnp.dot(att[here, :], wo[:, cols], preferred_element_type=jnp.float32)
                y = y.astype(jnp.bfloat16)
                for n, place in enumerate(blocks):
                    lead = n * 2 * ROWS
                    p0[rows_at(place), cols] = y[lead : lead + ROWS]
                    p1[rows_at(place), cols] = y[lead + ROWS : lead + 2 * ROWS]

        for place in blocks:
            part_over[place] = send(p1.at[rows_at(place)], s.at[place], sib)

    def total(dst, *terms):
        count = dst.shape[0] // 16

        @pl.loop(0, count)
        def _(i):
            rows = pl.ds(pl.multiple_of(i * 16, 16), 16)
            value = terms[0][rows, :].astype(jnp.float32)
            for term in terms[1:]:
                value = value + term[rows, :].astype(jnp.float32)
            dst[rows, :] = value.astype(jnp.bfloat16)

    a, b = pl.ds(0, X_COLS), pl.ds(X_COLS, D - X_COLS)
    x_first, hop_up, hop_down, end_up, end_down = {}, {}, {}, {}, {}

    def sum_at(place, cols, *terms, first=0, count=ROWS):
        dst = p0.at[rows_at(place, first, count), cols]
        total(dst, dst, *terms)

    def to_partner(z):
        place = PLACE[1, z]
        part_over[place].wait_recv()
        sum_at(place, a, s.at[place, :, a])
        x_first[z] = send(p0.at[rows_at(place), a], xf.at[z], x2)

    def first_hop(way, place, cols, r1, *terms):
        sum_at(place, cols, s.at[place, :, cols], *terms)
        hop_up[way] = send(p0.at[rows_at(place, 0, HALF), cols], r1.at[0], zp)
        hop_down[way] = send(p0.at[rows_at(place, HALF, HALF), cols], r1.at[1], zm)

    def second_hop(way, up, down, cols, r1, r2, up_terms=(), down_terms=()):
        sum_at(up, cols, s.at[up, :, cols], *up_terms)
        sum_at(down, cols, s.at[down, :, cols], *down_terms)
        hop_up[way].wait_recv()
        sum_at(up, cols, r1.at[0], count=HALF)
        end_up[way] = send(p0.at[rows_at(up), cols], r2.at[0], zp)
        hop_down[way].wait_recv()
        sum_at(down, cols, r1.at[1], first=HALF, count=HALF)
        end_down[way] = send(p0.at[rows_at(down), cols], r2.at[1], zm)

    finish(E_RIGHT, [7])
    finish(E_LEFT, [7])
    to_partner(2)
    first_hop(1, PLACE[1, 2], b, r1_b.at[1])
    finish(C, [5, 6, 7])
    part_over[PLACE[0, 2]].wait_recv()
    first_hop(0, PLACE[0, 2], b, r1_b.at[0])
    finish(B, [5, 6, 7])
    to_partner(1)
    to_partner(3)
    second_hop(1, PLACE[1, 1], PLACE[1, 3], b, r1_b.at[1], r2_b.at[1])
    finish(A, [5, 6, 7])
    to_partner(0)
    part_over[PLACE[0, 1]].wait_recv()
    part_over[PLACE[0, 3]].wait_recv()
    second_hop(0, PLACE[0, 1], PLACE[0, 3], b, r1_b.at[0], r2_b.at[0])
    x_first[2].wait_recv()
    first_hop(2, PLACE[0, 2], a, r1_a, xf.at[2])
    end_up[1].wait_recv()
    end_down[1].wait_recv()
    sum_at(1, b, s.at[1, :, b], r2_b.at[1, 0], r2_b.at[1, 1])
    last = send(p0.at[rows_at(1), b], xb, x2)
    x_first[1].wait_recv()
    x_first[3].wait_recv()
    second_hop(2, PLACE[0, 1], PLACE[0, 3], a, r1_a, r2_a, (xf.at[1],), (xf.at[3],))
    part_over[0].wait_recv()

    def renoise(cols, r2, partner):
        @pl.loop(0, ROWS // 16)
        def _(i):
            rows = pl.ds(pl.multiple_of(i * 16, 16), 16)
            mixed = p0[rows, cols].astype(jnp.float32) + s[0, rows, cols].astype(jnp.float32)
            mixed = mixed + r2[0, rows, :].astype(jnp.float32) + r2[1, rows, :].astype(jnp.float32)
            mixed = mixed + partner[rows, :].astype(jnp.float32)
            xrows = lat[rows, cols].astype(jnp.float32)
            fresh = noise[rows, cols].astype(jnp.float32)
            result = (1.0 - level_next) * (xrows - level_now * (xrows + mixed)) + level_next * fresh
            out[0, rows, cols] = result.astype(jnp.bfloat16)

    end_up[0].wait_recv()
    end_down[0].wait_recv()
    last.wait_recv()
    renoise(b, r2_b.at[0], xb)
    x_first[0].wait_recv()
    end_up[2].wait_recv()
    end_down[2].wait_recv()
    renoise(a, r2_a, xf.at[0])

    for copy in started:
        copy.wait_send()


def local(*operands):
    operands = operands[:9] + (operands[9].T,) + operands[10:]
    bf16, f32 = jnp.bfloat16, jnp.float32
    anywhere = pl.BlockSpec(memory_space=pl.ANY)
    vmem = pl.BlockSpec(memory_space=pltpu.VMEM)
    smem = pl.BlockSpec(memory_space=pltpu.SMEM)
    return pl.pallas_call(
        kernel,
        out_shape=jax.ShapeDtypeStruct((1, ROWS, D), bf16),
        in_specs=[anywhere] * 8 + [vmem] + [smem] * 4,
        out_specs=vmem,
        scratch_shapes=[
            pltpu.VMEM((ROWS, D), bf16),
            pltpu.VMEM((ROWS, D), bf16),
            pltpu.VMEM((3, D, W), bf16),
            pltpu.VMEM((W, D), bf16),
            pltpu.VMEM((TOK, D), bf16),
            pltpu.VMEM((9, 2, TOK, W), bf16),
            pltpu.VMEM((TOK, W), bf16),
            pltpu.VMEM((TOK, 2 * W), f32),
            pltpu.VMEM((TOK, W), f32),
            pltpu.VMEM((2 * 2 * ROWS, W), bf16),
            pltpu.VMEM((8, ROWS, D), bf16),
            pltpu.VMEM((2, HALF, X_COLS), bf16),
            pltpu.VMEM((2, 2, HALF, D - X_COLS), bf16),
            pltpu.VMEM((2, ROWS, X_COLS), bf16),
            pltpu.VMEM((2, 2, ROWS, D - X_COLS), bf16),
            pltpu.VMEM((4, ROWS, X_COLS), bf16),
            pltpu.VMEM((ROWS, D - X_COLS), bf16),
            pltpu.SMEM((16,), jnp.int32),
            pltpu.SemaphoreType.DMA((8,)),
            pltpu.SemaphoreType.DMA((N_SEM,)),
            pltpu.SemaphoreType.DMA((N_SEM,)),
        ],
        compiler_params=pltpu.CompilerParams(
            collective_id=0, has_side_effects=True, vmem_limit_bytes=62 * 2**20
        ),
    )(*operands)


def solution(mesh):
    in_specs = (
        P("span", "seq", None),
        P("span", "seq", None),
        P("span", None, "seq"),
        P("span", None, "seq"),
        P(None, "seq"),
        P(None, "seq"),
        P(None, "seq"),
        P("seq", None),
        P(),
        P(),
        P(),
        P(),
        P(),
    )
    out_specs = P("span", "seq", None)
    return jax.shard_map(local, mesh=mesh, in_specs=in_specs, out_specs=out_specs, check_vma=False)
```

```python
import itertools

import jax
import jax.numpy as jnp
from jax import lax
from jax.experimental import pallas as pl
from jax.experimental.pallas import tpu as pltpu
from jax.sharding import PartitionSpec as P

HD = 128
D = 5120
TOK = 1024
W = 256
ROWS = 64
HALF = 32
PIECES = ((0, 240), (240, 240), (480, 224), (704, 320))
X_COLS = 2304
LOG2E = 1.4426950408889634
SCALE = LOG2E / HD**0.5
LOW = -1e30
HIGH = 3e38
MESH = pl.DeviceIdType.MESH
N_SEM = 144

PLACE = {(0, 0): 0, (1, 0): 1, (0, 1): 2, (0, 3): 3, (1, 1): 4, (1, 3): 5, (0, 2): 6, (1, 2): 7}
CACHE = {(0, 0): 0, (0, 1): 1, (0, 3): 2, (1, 0): 3, (1, 1): 4, (1, 3): 5, (0, 2): 6, (1, 2): 7}
OWN = 8
A, B, C, E = (0, 256), (256, 256), (512, 256), (768, 256)
E_LEFT, E_RIGHT = (768, 128), (896, 128)


def kernel(
    latent_hbm,
    noise_hbm,
    ck_hbm,
    cv_hbm,
    wq_hbm,
    wk_hbm,
    wv_hbm,
    wo_hbm,
    modulation,
    plan,
    step_index,
    assignment,
    visible,
    out,
    lat,
    noise,
    w,
    wo,
    g,
    kv,
    q,
    acc,
    top,
    att,
    s,
    r1_a,
    r1_b,
    r2_a,
    r2_b,
    xf,
    xb,
    flags,
    local_sem,
    send_sem,
    recv_sem,
):
    span = lax.axis_index("span")
    seq = lax.axis_index("seq")
    x_lo = span // 4
    y = span % 4
    x_hi = seq // 8
    z = (seq // 2) % 4
    core = seq % 2

    def seq_of(a, b, c):
        return a * 8 + b * 2 + c

    sib = (span, seq_of(x_hi, z, 1 - core))
    x2 = (span, seq_of(1 - x_hi, z, core))
    zp = (span, seq_of(x_hi, (z + 1) % 4, core))
    zm = (span, seq_of(x_hi, (z + 3) % 4, core))
    xn = ((1 - x_lo) * 4 + y, seq)
    yp = (x_lo * 4 + (y + 1) % 4, seq)
    ym = (x_lo * 4 + (y + 3) % 4, seq)

    loads = {}
    for i, (name, src, dst) in enumerate(
        (
            ("k", ck_hbm.at[0], kv.at[0, 0]),
            ("v", cv_hbm.at[0], kv.at[0, 1]),
            ("lat", latent_hbm.at[0], lat),
            ("wq", wq_hbm, w.at[0]),
            ("wk", wk_hbm, w.at[1]),
            ("wv", wv_hbm, w.at[2]),
            ("wo", wo_hbm, wo),
            ("noise", noise_hbm.at[0], noise),
        )
    ):
        loads[name] = pltpu.make_async_copy(src, dst, local_sem.at[i])
        loads[name].start()

    barrier = pltpu.get_barrier_semaphore()
    for device in (sib, x2, zp, zm, xn, yp, ym):
        pl.semaphore_signal(barrier, 1, device_id=device, device_id_type=MESH)
    started = []
    count = itertools.count()

    def send(src, dst, device):
        i = next(count)
        copy = pltpu.make_async_remote_copy(
            src, dst, send_sem.at[i], recv_sem.at[i], device_id=device, device_id_type=MESH
        )
        copy.start()
        started.append(copy)
        return copy

    def piece(place, j):
        return kv.at[place, :, pl.ds(*PIECES[j])]

    def part(place, side, j):
        return kv.at[place, side, pl.ds(*PIECES[j])]

    def send_piece(src, dst, j, device):
        return send(piece(CACHE[src], j), piece(CACHE[dst], j), device)

    def rows_of(place, sub, half=None):
        base = PLACE[place] * 2 * ROWS + sub * ROWS
        if half is None:
            return g.at[pl.ds(base, ROWS)]
        return g.at[pl.ds(base + half * HALF, HALF)]

    step = step_index[span]
    level_now = plan[0, step]
    level_next = plan[1, step]
    loads["lat"].wait()

    @pl.loop(0, 4)
    def _(i):
        rows = pl.ds(pl.multiple_of(i * 16, 16), 16)
        values = lat[rows, :].astype(jnp.float32)
        rms = lax.rsqrt(jnp.mean(values * values, axis=1, keepdims=True) + 1e-06)
        shift = modulation[step, 0:1, :]
        scale = modulation[step, 1:2, :]
        g[rows, :] = (values * rms * (1.0 + scale) + shift).astype(jnp.bfloat16)

    mine = assignment[span]
    for (dx, dy), place in CACHE.items():
        other = ((x_lo + dx) % 2) * 4 + (y + dy) % 4
        flags[place] = visible[mine, assignment[other]]
    flags[OWN] = 1

    acc[...] = jnp.zeros_like(acc)
    top[...] = jnp.full_like(top, LOW)

    pl.semaphore_wait(barrier, 7)
    x_part, z_up, z_down, over = {}, {}, {}, {}
    for h in range(2):
        x_part[h] = send(rows_of((0, 0), 0, h), rows_of((1, 0), 0, h), x2)
    for h in range(2):
        z_up[0, h] = send(rows_of((0, 0), 0, h), rows_of((0, 3), 0, h), zp)
        z_down[0, h] = send(rows_of((0, 0), 0, h), rows_of((0, 1), 0, h), zm)

    def to_sibling(place):
        over[place] = send(rows_of(place, 0), rows_of(place, 1), sib)

    to_sibling((0, 0))

    loads["k"].wait()
    loads["v"].wait()
    y_up, y_down, x_over = {}, {}, {}
    for j in range(4):
        y_up[0, j] = send_piece((0, 0), (0, 3), j, yp)
        y_down[0, j] = send_piece((0, 0), (0, 1), j, ym)
    for j in range(3):
        x_over[0, j] = send_piece((0, 0), (1, 0), j, xn)

    for h in range(2):
        x_part[h].wait_recv()
        z_up[1, h] = send(rows_of((1, 0), 0, h), rows_of((1, 3), 0, h), zp)
        z_down[1, h] = send(rows_of((1, 0), 0, h), rows_of((1, 1), 0, h), zm)
    to_sibling((1, 0))
    def project(group):
        rows = pl.ds(*group)

        @pl.loop(0, 3)
        def _(i):
            y = jnp.dot(g[rows, :], w[i], preferred_element_type=jnp.float32)
            y = (y * jnp.where(i == 0, SCALE, 1.0)).astype(jnp.bfloat16)

            @pl.when(i == 0)
            def _():
                q[rows, :] = y

            @pl.when(i > 0)
            def _():
                kv[OWN, i - 1, rows, :] = y

    ones = jnp.ones((TOK, HD), jnp.bfloat16)

    def attend(groups, places):
        items = [(pl.ds(*group), h) for group in groups for h in range(W // HD)]
        seen = [jnp.full((8, HD), flags[place], jnp.int32) > 0 for place in places]
        seen = [{count: jnp.tile(mark, (count // 8, 1)) for _, count in groups} for mark in seen]
        olds = [top[rows, h * HD : (h + 1) * HD] for rows, h in items]
        scores, results = {}, {}

        def score(i):
            rows, h = items[i]
            cols = slice(h * HD, (h + 1) * HD)
            scores[i] = [
                lax.dot_general(
                    q[rows, cols],
                    kv[place, 0, :, cols],
                    (((1,), (1,)), ((), ())),
                    preferred_element_type=jnp.float32,
                )
                for place in places
            ]

        def weigh(i):
            rows, h = items[i]
            cols = slice(h * HD, (h + 1) * HD)
            new = olds[i]
            marks = [mark[rows.size] for mark in seen]
            for mark, block in zip(marks, scores[i]):
                new = jnp.where(mark, jnp.maximum(new, jnp.max(block, axis=1, keepdims=True)), new)
            shrink = jnp.exp2(olds[i] - new)
            lead = h * 2 * HD
            value = acc[rows, lead : lead + HD] * shrink
            total = acc[rows, lead + HD : lead + 2 * HD] * shrink
            for mark, block, place in zip(marks, scores[i], places):
                low = jnp.where(mark, new, HIGH)
                weights = jnp.exp2(block - jnp.tile(low, (1, TOK // HD))).astype(jnp.bfloat16)
                both = jnp.concatenate((kv[place, 1, :, cols], ones), axis=1)
                sums = jnp.dot(weights, both, preferred_element_type=jnp.float32)
                value = value + sums[:, :HD]
                total = total + sums[:, HD:]
            results[i] = (new, value, total)

        score(0)
        for i in range(len(items)):
            if i + 1 < len(items):
                score(i + 1)
            weigh(i)
        for i, (rows, h) in enumerate(items):
            lead = h * 2 * HD
            top[rows, h * HD : (h + 1) * HD], acc[rows, lead : lead + HD], acc[rows, lead + HD : lead + 2 * HD] = (
                results[i]
            )

    z_fwd_up, z_fwd_down = {}, {}

    def forward_z(x):
        for h in range(2):
            z_up[x, h].wait_recv()
            z_down[x, h].wait_recv()
        z_fwd_up[x] = send(rows_of((x, 3), 0, 0), rows_of((x, 2), 0, 0), zp)
        z_fwd_down[x] = send(rows_of((x, 1), 0, 1), rows_of((x, 2), 0, 1), zm)
        to_sibling((x, 3))
        to_sibling((x, 1))

    y_fwd_up, y_fwd_down = {}, {}

    def forward_y(x, j):
        y_fwd_up[x, j] = send(part(CACHE[x, 3], 0, j), part(CACHE[x, 2], 0, j), yp)
        y_fwd_down[x, j] = send(part(CACHE[x, 1], 1, j), part(CACHE[x, 2], 1, j), ym)

    def forward_x(j):
        x_over[0, j].wait_recv()
        y_up[1, j] = send_piece((1, 0), (1, 3), j, yp)
        y_down[1, j] = send_piece((1, 0), (1, 1), j, ym)

    forward_z(0)
    for name in ("wq", "wk", "wv"):
        loads[name].wait()
    over[0, 0].wait_recv()
    over[1, 0].wait_recv()
    forward_x(0)
    project(A)
    over[0, 1].wait_recv()
    over[0, 3].wait_recv()
    project(B)
    attend([A, B], [0])
    for j in range(4):
        y_up[0, j].wait_recv()
        y_down[0, j].wait_recv()
    forward_x(1)
    for dy in (0, 1, 3):
        x_over[dy, 3] = send_piece((0, dy), (1, dy), 3, xn)

    @pl.loop(1, 3)
    def _(place):
        attend([A, B], [place])

    forward_x(2)
    for j in (3, 0, 1, 2):
        forward_y(0, j)
    forward_z(1)
    over[1, 1].wait_recv()
    over[1, 3].wait_recv()
    project(C)
    attend([C], [0, 1])
    z_fwd_up[0].wait_recv()
    z_fwd_down[0].wait_recv()
    to_sibling((0, 2))
    x_over[0, 3].wait_recv()
    attend([A, B], [3])
    attend([C], [2, 3])
    over[0, 2].wait_recv()
    project(E_LEFT)
    for j in range(3):
        y_up[1, j].wait_recv()
        y_down[1, j].wait_recv()
        forward_y(1, j)
    y_fwd_up[0, 3].wait_recv()
    y_fwd_down[0, 3].wait_recv()
    x_over[2, 3] = send_piece((0, 2), (1, 2), 3, xn)
    z_fwd_up[1].wait_recv()
    z_fwd_down[1].wait_recv()
    to_sibling((1, 2))
    attend([E_LEFT], [0, 1, 2, 3])
    x_over[1, 3].wait_recv()
    attend([A, B, C, E_LEFT], [4])
    over[1, 2].wait_recv()
    project(E_RIGHT)
    attend([E_RIGHT], [0, 1, 2, 3, 4])
    attend([A, B, C, E], [OWN])
    x_over[3, 3].wait_recv()
    for j in range(3):
        y_fwd_up[0, j].wait_recv()
        y_fwd_down[0, j].wait_recv()

    attend([E], [5, 6])
    for j in range(3):
        y_fwd_up[1, j].wait_recv()
        y_fwd_down[1, j].wait_recv()
    x_over[2, 3].wait_recv()
    loads["wo"].wait()
    loads["noise"].wait()

    for copy in started:
        copy.wait_send()
    started.clear()
    p0 = g.at[pl.ds(0, 8 * ROWS)]
    p1 = g.at[pl.ds(8 * ROWS, 8 * ROWS)]
    part_over = {}

    def rows_at(place, first=0, count=ROWS):
        return pl.ds(place * ROWS + first, count)

    def finish(group, places):
        attend([group], places)
        start, count = group
        rows, here = pl.ds(start, count), pl.ds(0, count)
        for h in range(W // HD):
            lead = h * 2 * HD
            att[here, h * HD : (h + 1) * HD] = (
                acc[rows, lead : lead + HD] / acc[rows, lead + HD : lead + 2 * HD]
            ).astype(jnp.bfloat16)
        blocks = range(start // (2 * ROWS), (start + count) // (2 * ROWS))

        @pl.loop(0, 2)
        def _(i):
            for k in range(5):
                cols = pl.ds(pl.multiple_of(i * (D // 2) + k * 512, 512), 512)
                y = jnp.dot(att[here, :], wo[:, cols], preferred_element_type=jnp.float32)
                y = y.astype(jnp.bfloat16)
                for n, place in enumerate(blocks):
                    lead = n * 2 * ROWS
                    p0[rows_at(place), cols] = y[lead : lead + ROWS]
                    p1[rows_at(place), cols] = y[lead + ROWS : lead + 2 * ROWS]

        for place in blocks:
            part_over[place] = send(p1.at[rows_at(place)], s.at[place], sib)

    def total(dst, *terms):
        count = dst.shape[0] // 16

        @pl.loop(0, count)
        def _(i):
            rows = pl.ds(pl.multiple_of(i * 16, 16), 16)
            value = terms[0][rows, :].astype(jnp.float32)
            for term in terms[1:]:
                value = value + term[rows, :].astype(jnp.float32)
            dst[rows, :] = value.astype(jnp.bfloat16)

    a, b = pl.ds(0, X_COLS), pl.ds(X_COLS, D - X_COLS)
    x_first, hop_up, hop_down, end_up, end_down = {}, {}, {}, {}, {}

    def sum_at(place, cols, *terms, first=0, count=ROWS):
        dst = p0.at[rows_at(place, first, count), cols]
        total(dst, dst, *terms)

    def to_partner(z):
        place = PLACE[1, z]
        part_over[place].wait_recv()
        sum_at(place, a, s.at[place, :, a])
        x_first[z] = send(p0.at[rows_at(place), a], xf.at[z], x2)

    def first_hop(way, place, cols, r1, *terms):
        sum_at(place, cols, s.at[place, :, cols], *terms)
        hop_up[way] = send(p0.at[rows_at(place, 0, HALF), cols], r1.at[0], zp)
        hop_down[way] = send(p0.at[rows_at(place, HALF, HALF), cols], r1.at[1], zm)

    def second_hop(way, up, down, cols, r1, r2, up_terms=(), down_terms=()):
        sum_at(up, cols, s.at[up, :, cols], *up_terms)
        sum_at(down, cols, s.at[down, :, cols], *down_terms)
        hop_up[way].wait_recv()
        sum_at(up, cols, r1.at[0], count=HALF)
        end_up[way] = send(p0.at[rows_at(up), cols], r2.at[0], zp)
        hop_down[way].wait_recv()
        sum_at(down, cols, r1.at[1], first=HALF, count=HALF)
        end_down[way] = send(p0.at[rows_at(down), cols], r2.at[1], zm)

    finish(E_RIGHT, [7])
    finish(E_LEFT, [7])
    to_partner(2)
    first_hop(1, PLACE[1, 2], b, r1_b.at[1])
    finish(C, [5, 6, 7])
    part_over[PLACE[0, 2]].wait_recv()
    first_hop(0, PLACE[0, 2], b, r1_b.at[0])
    finish(B, [5, 6, 7])
    to_partner(1)
    to_partner(3)
    second_hop(1, PLACE[1, 1], PLACE[1, 3], b, r1_b.at[1], r2_b.at[1])
    finish(A, [5, 6, 7])
    to_partner(0)
    part_over[PLACE[0, 1]].wait_recv()
    part_over[PLACE[0, 3]].wait_recv()
    second_hop(0, PLACE[0, 1], PLACE[0, 3], b, r1_b.at[0], r2_b.at[0])
    x_first[2].wait_recv()
    first_hop(2, PLACE[0, 2], a, r1_a, xf.at[2])
    end_up[1].wait_recv()
    end_down[1].wait_recv()
    sum_at(1, b, s.at[1, :, b], r2_b.at[1, 0], r2_b.at[1, 1])
    last = send(p0.at[rows_at(1), b], xb, x2)
    x_first[1].wait_recv()
    x_first[3].wait_recv()
    second_hop(2, PLACE[0, 1], PLACE[0, 3], a, r1_a, r2_a, (xf.at[1],), (xf.at[3],))
    part_over[0].wait_recv()

    def renoise(cols, r2, partner):
        @pl.loop(0, ROWS // 16)
        def _(i):
            rows = pl.ds(pl.multiple_of(i * 16, 16), 16)
            mixed = p0[rows, cols].astype(jnp.float32) + s[0, rows, cols].astype(jnp.float32)
            mixed = mixed + r2[0, rows, :].astype(jnp.float32) + r2[1, rows, :].astype(jnp.float32)
            mixed = mixed + partner[rows, :].astype(jnp.float32)
            xrows = lat[rows, cols].astype(jnp.float32)
            fresh = noise[rows, cols].astype(jnp.float32)
            result = (1.0 - level_next) * (xrows - level_now * (xrows + mixed)) + level_next * fresh
            out[0, rows, cols] = result.astype(jnp.bfloat16)

    end_up[0].wait_recv()
    end_down[0].wait_recv()
    last.wait_recv()
    renoise(b, r2_b.at[0], xb)
    x_first[0].wait_recv()
    end_up[2].wait_recv()
    end_down[2].wait_recv()
    renoise(a, r2_a, xf.at[0])

    for copy in started:
        copy.wait_send()


def local(*operands):
    operands = operands[:9] + (operands[9].T,) + operands[10:]
    bf16, f32 = jnp.bfloat16, jnp.float32
    anywhere = pl.BlockSpec(memory_space=pl.ANY)
    vmem = pl.BlockSpec(memory_space=pltpu.VMEM)
    smem = pl.BlockSpec(memory_space=pltpu.SMEM)
    return pl.pallas_call(
        kernel,
        out_shape=jax.ShapeDtypeStruct((1, ROWS, D), bf16),
        in_specs=[anywhere] * 8 + [vmem] + [smem] * 4,
        out_specs=vmem,
        scratch_shapes=[
            pltpu.VMEM((ROWS, D), bf16),
            pltpu.VMEM((ROWS, D), bf16),
            pltpu.VMEM((3, D, W), bf16),
            pltpu.VMEM((W, D), bf16),
            pltpu.VMEM((TOK, D), bf16),
            pltpu.VMEM((9, 2, TOK, W), bf16),
            pltpu.VMEM((TOK, W), bf16),
            pltpu.VMEM((TOK, 2 * W), f32),
            pltpu.VMEM((TOK, W), f32),
            pltpu.VMEM((2 * 2 * ROWS, W), bf16),
            pltpu.VMEM((8, ROWS, D), bf16),
            pltpu.VMEM((2, HALF, X_COLS), bf16),
            pltpu.VMEM((2, 2, HALF, D - X_COLS), bf16),
            pltpu.VMEM((2, ROWS, X_COLS), bf16),
            pltpu.VMEM((2, 2, ROWS, D - X_COLS), bf16),
            pltpu.VMEM((4, ROWS, X_COLS), bf16),
            pltpu.VMEM((ROWS, D - X_COLS), bf16),
            pltpu.SMEM((16,), jnp.int32),
            pltpu.SemaphoreType.DMA((8,)),
            pltpu.SemaphoreType.DMA((N_SEM,)),
            pltpu.SemaphoreType.DMA((N_SEM,)),
        ],
        compiler_params=pltpu.CompilerParams(
            collective_id=0, has_side_effects=True, vmem_limit_bytes=62 * 2**20
        ),
    )(*operands)


def solution(mesh):
    in_specs = (
        P("span", "seq", None),
        P("span", "seq", None),
        P("span", None, "seq"),
        P("span", None, "seq"),
        P(None, "seq"),
        P(None, "seq"),
        P(None, "seq"),
        P("seq", None),
        P(),
        P(),
        P(),
        P(),
        P(),
    )
    out_specs = P("span", "seq", None)
    return jax.shard_map(local, mesh=mesh, in_specs=in_specs, out_specs=out_specs, check_vma=False)
```

```python
import itertools

import jax
import jax.numpy as jnp
from jax import lax
from jax.experimental import pallas as pl
from jax.experimental.pallas import tpu as pltpu
from jax.sharding import PartitionSpec as P

HD = 128
D = 5120
TOK = 1024
W = 256
ROWS = 64
HALF = 32
PIECES = ((0, 240), (240, 240), (480, 224), (704, 320))
X_COLS = 2304
LOG2E = 1.4426950408889634
SCALE = LOG2E / HD**0.5
LOW = -1e30
HIGH = 3e38
MESH = pl.DeviceIdType.MESH
N_SEM = 144

PLACE = {(0, 0): 0, (1, 0): 1, (0, 1): 2, (0, 3): 3, (1, 1): 4, (1, 3): 5, (0, 2): 6, (1, 2): 7}
CACHE = {(0, 0): 0, (0, 1): 1, (0, 3): 2, (1, 0): 3, (1, 1): 4, (1, 3): 5, (0, 2): 6, (1, 2): 7}
OWN = 8
A, B, C, E = (0, 256), (256, 256), (512, 256), (768, 256)
E_LEFT, E_RIGHT = (768, 128), (896, 128)


def kernel(
    latent_hbm,
    noise_hbm,
    ck_hbm,
    cv_hbm,
    wq_hbm,
    wk_hbm,
    wv_hbm,
    wo_hbm,
    modulation,
    plan,
    step_index,
    assignment,
    visible,
    out,
    lat,
    noise,
    w,
    wo,
    g,
    kv,
    q,
    acc,
    top,
    att,
    s,
    r1_a,
    r1_b,
    r2_a,
    r2_b,
    xf,
    xb,
    flags,
    local_sem,
    send_sem,
    recv_sem,
):
    span = lax.axis_index("span")
    seq = lax.axis_index("seq")
    x_lo = span // 4
    y = span % 4
    x_hi = seq // 8
    z = (seq // 2) % 4
    core = seq % 2

    def seq_of(a, b, c):
        return a * 8 + b * 2 + c

    sib = (span, seq_of(x_hi, z, 1 - core))
    x2 = (span, seq_of(1 - x_hi, z, core))
    zp = (span, seq_of(x_hi, (z + 1) % 4, core))
    zm = (span, seq_of(x_hi, (z + 3) % 4, core))
    xn = ((1 - x_lo) * 4 + y, seq)
    yp = (x_lo * 4 + (y + 1) % 4, seq)
    ym = (x_lo * 4 + (y + 3) % 4, seq)

    loads = {}
    for i, (name, src, dst) in enumerate(
        (
            ("k", ck_hbm.at[0], kv.at[0, 0]),
            ("v", cv_hbm.at[0], kv.at[0, 1]),
            ("lat", latent_hbm.at[0], lat),
            ("wq", wq_hbm, w.at[0]),
            ("wk", wk_hbm, w.at[1]),
            ("wv", wv_hbm, w.at[2]),
            ("wo", wo_hbm, wo),
            ("noise", noise_hbm.at[0], noise),
        )
    ):
        loads[name] = pltpu.make_async_copy(src, dst, local_sem.at[i])
        loads[name].start()

    barrier = pltpu.get_barrier_semaphore()
    for device in (sib, x2, zp, zm, xn, yp, ym):
        pl.semaphore_signal(barrier, 1, device_id=device, device_id_type=MESH)
    started = []
    count = itertools.count()

    def send(src, dst, device):
        i = next(count)
        copy = pltpu.make_async_remote_copy(
            src, dst, send_sem.at[i], recv_sem.at[i], device_id=device, device_id_type=MESH
        )
        copy.start()
        started.append(copy)
        return copy

    def piece(place, j):
        return kv.at[place, :, pl.ds(*PIECES[j])]

    def part(place, side, j):
        return kv.at[place, side, pl.ds(*PIECES[j])]

    def send_piece(src, dst, j, device):
        return send(piece(CACHE[src], j), piece(CACHE[dst], j), device)

    def rows_of(place, sub, half=None):
        base = PLACE[place] * 2 * ROWS + sub * ROWS
        if half is None:
            return g.at[pl.ds(base, ROWS)]
        return g.at[pl.ds(base + half * HALF, HALF)]

    step = step_index[span]
    level_now = plan[0, step]
    level_next = plan[1, step]
    loads["lat"].wait()

    @pl.loop(0, 4)
    def _(i):
        rows = pl.ds(pl.multiple_of(i * 16, 16), 16)
        values = lat[rows, :].astype(jnp.float32)
        rms = lax.rsqrt(jnp.mean(values * values, axis=1, keepdims=True) + 1e-06)
        shift = modulation[step, 0:1, :]
        scale = modulation[step, 1:2, :]
        g[rows, :] = (values * rms * (1.0 + scale) + shift).astype(jnp.bfloat16)

    mine = assignment[span]
    for (dx, dy), place in CACHE.items():
        other = ((x_lo + dx) % 2) * 4 + (y + dy) % 4
        flags[place] = visible[mine, assignment[other]]
    flags[OWN] = 1

    acc[...] = jnp.zeros_like(acc)
    top[...] = jnp.full_like(top, LOW)

    pl.semaphore_wait(barrier, 7)
    x_part, z_up, z_down, over = {}, {}, {}, {}
    for h in range(2):
        x_part[h] = send(rows_of((0, 0), 0, h), rows_of((1, 0), 0, h), x2)
    for h in range(2):
        z_up[0, h] = send(rows_of((0, 0), 0, h), rows_of((0, 3), 0, h), zp)
        z_down[0, h] = send(rows_of((0, 0), 0, h), rows_of((0, 1), 0, h), zm)

    def to_sibling(place):
        over[place] = send(rows_of(place, 0), rows_of(place, 1), sib)

    to_sibling((0, 0))

    loads["k"].wait()
    loads["v"].wait()
    y_up, y_down, x_over = {}, {}, {}
    for j in range(4):
        y_up[0, j] = send_piece((0, 0), (0, 3), j, yp)
        y_down[0, j] = send_piece((0, 0), (0, 1), j, ym)
    for j in range(3):
        x_over[0, j] = send_piece((0, 0), (1, 0), j, xn)

    for h in range(2):
        x_part[h].wait_recv()
        z_up[1, h] = send(rows_of((1, 0), 0, h), rows_of((1, 3), 0, h), zp)
        z_down[1, h] = send(rows_of((1, 0), 0, h), rows_of((1, 1), 0, h), zm)
    to_sibling((1, 0))
    def project(group):
        rows = pl.ds(*group)

        @pl.loop(0, 3)
        def _(i):
            y = jnp.dot(g[rows, :], w[i], preferred_element_type=jnp.float32)
            y = (y * jnp.where(i == 0, SCALE, 1.0)).astype(jnp.bfloat16)

            @pl.when(i == 0)
            def _():
                q[rows, :] = y

            @pl.when(i > 0)
            def _():
                kv[OWN, i - 1, rows, :] = y

    ones = jnp.ones((TOK, HD), jnp.bfloat16)

    def attend(groups, places):
        items = [(pl.ds(*group), h) for group in groups for h in range(W // HD)]
        seen = [jnp.full((8, HD), flags[place], jnp.int32) > 0 for place in places]
        seen = [{count: jnp.tile(mark, (count // 8, 1)) for _, count in groups} for mark in seen]
        olds = [top[rows, h * HD : (h + 1) * HD] for rows, h in items]
        scores, results = {}, {}

        def score(i):
            rows, h = items[i]
            cols = slice(h * HD, (h + 1) * HD)
            scores[i] = [
                lax.dot_general(
                    q[rows, cols],
                    kv[place, 0, :, cols],
                    (((1,), (1,)), ((), ())),
                    preferred_element_type=jnp.float32,
                )
                for place in places
            ]

        def weigh(i):
            rows, h = items[i]
            cols = slice(h * HD, (h + 1) * HD)
            new = olds[i]
            marks = [mark[rows.size] for mark in seen]
            for mark, block in zip(marks, scores[i]):
                new = jnp.where(mark, jnp.maximum(new, jnp.max(block, axis=1, keepdims=True)), new)
            shrink = jnp.exp2(olds[i] - new)
            lead = h * 2 * HD
            value = acc[rows, lead : lead + HD] * shrink
            total = acc[rows, lead + HD : lead + 2 * HD] * shrink
            for mark, block, place in zip(marks, scores[i], places):
                low = jnp.where(mark, new, HIGH)
                weights = jnp.exp2(block - jnp.tile(low, (1, TOK // HD))).astype(jnp.bfloat16)
                both = jnp.concatenate((kv[place, 1, :, cols], ones), axis=1)
                sums = jnp.dot(weights, both, preferred_element_type=jnp.float32)
                value = value + sums[:, :HD]
                total = total + sums[:, HD:]
            results[i] = (new, value, total)

        score(0)
        for i in range(len(items)):
            if i + 1 < len(items):
                score(i + 1)
            weigh(i)
        for i, (rows, h) in enumerate(items):
            lead = h * 2 * HD
            top[rows, h * HD : (h + 1) * HD], acc[rows, lead : lead + HD], acc[rows, lead + HD : lead + 2 * HD] = (
                results[i]
            )

    z_fwd_up, z_fwd_down = {}, {}

    def forward_z(x):
        for h in range(2):
            z_up[x, h].wait_recv()
            z_down[x, h].wait_recv()
        z_fwd_up[x] = send(rows_of((x, 3), 0, 0), rows_of((x, 2), 0, 0), zp)
        z_fwd_down[x] = send(rows_of((x, 1), 0, 1), rows_of((x, 2), 0, 1), zm)
        to_sibling((x, 3))
        to_sibling((x, 1))

    y_fwd_up, y_fwd_down = {}, {}

    def forward_y(x, j):
        y_fwd_up[x, j] = send(part(CACHE[x, 3], 0, j), part(CACHE[x, 2], 0, j), yp)
        y_fwd_down[x, j] = send(part(CACHE[x, 1], 1, j), part(CACHE[x, 2], 1, j), ym)

    def forward_x(j):
        x_over[0, j].wait_recv()
        y_up[1, j] = send_piece((1, 0), (1, 3), j, yp)
        y_down[1, j] = send_piece((1, 0), (1, 1), j, ym)

    forward_z(0)
    for name in ("wq", "wk", "wv"):
        loads[name].wait()
    over[0, 0].wait_recv()
    over[1, 0].wait_recv()
    forward_x(0)
    project(A)
    over[0, 1].wait_recv()
    over[0, 3].wait_recv()
    project(B)
    attend([A, B], [0])
    for j in range(4):
        y_up[0, j].wait_recv()
        y_down[0, j].wait_recv()
    forward_x(1)
    for dy in (0, 1, 3):
        x_over[dy, 3] = send_piece((0, dy), (1, dy), 3, xn)

    @pl.loop(1, 3)
    def _(place):
        attend([A, B], [place])

    forward_x(2)
    for j in (3, 0, 1, 2):
        forward_y(0, j)
    forward_z(1)
    over[1, 1].wait_recv()
    over[1, 3].wait_recv()
    project(C)
    attend([C], [0, 1])
    z_fwd_up[0].wait_recv()
    z_fwd_down[0].wait_recv()
    to_sibling((0, 2))
    x_over[0, 3].wait_recv()
    attend([A, B], [3])
    attend([C], [2, 3])
    over[0, 2].wait_recv()
    project(E_LEFT)
    for j in range(3):
        y_up[1, j].wait_recv()
        y_down[1, j].wait_recv()
        forward_y(1, j)
    y_fwd_up[0, 3].wait_recv()
    y_fwd_down[0, 3].wait_recv()
    x_over[2, 3] = send_piece((0, 2), (1, 2), 3, xn)
    z_fwd_up[1].wait_recv()
    z_fwd_down[1].wait_recv()
    to_sibling((1, 2))
    attend([E_LEFT], [0, 1, 2, 3])
    x_over[1, 3].wait_recv()
    attend([A, B, C, E_LEFT], [4])
    over[1, 2].wait_recv()
    project(E_RIGHT)
    attend([E_RIGHT], [0, 1, 2, 3, 4])
    attend([A, B, C, E], [OWN])
    x_over[3, 3].wait_recv()
    for j in range(3):
        y_fwd_up[0, j].wait_recv()
        y_fwd_down[0, j].wait_recv()

    attend([E], [5, 6])
    for j in range(3):
        y_fwd_up[1, j].wait_recv()
        y_fwd_down[1, j].wait_recv()
    x_over[2, 3].wait_recv()
    loads["wo"].wait()
    loads["noise"].wait()

    for copy in started:
        copy.wait_send()
    started.clear()
    p0 = g.at[pl.ds(0, 8 * ROWS)]
    p1 = g.at[pl.ds(8 * ROWS, 8 * ROWS)]
    part_over = {}

    def rows_at(place, first=0, count=ROWS):
        return pl.ds(place * ROWS + first, count)

    def finish(group, places):
        attend([group], places)
        start, count = group
        rows, here = pl.ds(start, count), pl.ds(0, count)
        for h in range(W // HD):
            lead = h * 2 * HD
            att[here, h * HD : (h + 1) * HD] = (
                acc[rows, lead : lead + HD] / acc[rows, lead + HD : lead + 2 * HD]
            ).astype(jnp.bfloat16)
        blocks = range(start // (2 * ROWS), (start + count) // (2 * ROWS))

        @pl.loop(0, 2)
        def _(i):
            for k in range(5):
                cols = pl.ds(pl.multiple_of(i * (D // 2) + k * 512, 512), 512)
                y = jnp.dot(att[here, :], wo[:, cols], preferred_element_type=jnp.float32)
                y = y.astype(jnp.bfloat16)
                for n, place in enumerate(blocks):
                    lead = n * 2 * ROWS
                    p0[rows_at(place), cols] = y[lead : lead + ROWS]
                    p1[rows_at(place), cols] = y[lead + ROWS : lead + 2 * ROWS]

        for place in blocks:
            part_over[place] = send(p1.at[rows_at(place)], s.at[place], sib)

    def total(dst, *terms):
        count = dst.shape[0] // 16

        @pl.loop(0, count)
        def _(i):
            rows = pl.ds(pl.multiple_of(i * 16, 16), 16)
            value = terms[0][rows, :].astype(jnp.float32)
            for term in terms[1:]:
                value = value + term[rows, :].astype(jnp.float32)
            dst[rows, :] = value.astype(jnp.bfloat16)

    a, b = pl.ds(0, X_COLS), pl.ds(X_COLS, D - X_COLS)
    x_first, hop_up, hop_down, end_up, end_down = {}, {}, {}, {}, {}

    def sum_at(place, cols, *terms, first=0, count=ROWS):
        dst = p0.at[rows_at(place, first, count), cols]
        total(dst, dst, *terms)

    def to_partner(z):
        place = PLACE[1, z]
        part_over[place].wait_recv()
        sum_at(place, a, s.at[place, :, a])
        x_first[z] = send(p0.at[rows_at(place), a], xf.at[z], x2)

    def first_hop(way, place, cols, r1, *terms):
        sum_at(place, cols, s.at[place, :, cols], *terms)
        hop_up[way] = send(p0.at[rows_at(place, 0, HALF), cols], r1.at[0], zp)
        hop_down[way] = send(p0.at[rows_at(place, HALF, HALF), cols], r1.at[1], zm)

    def second_hop(way, up, down, cols, r1, r2, up_terms=(), down_terms=()):
        sum_at(up, cols, s.at[up, :, cols], *up_terms)
        sum_at(down, cols, s.at[down, :, cols], *down_terms)
        hop_up[way].wait_recv()
        sum_at(up, cols, r1.at[0], count=HALF)
        end_up[way] = send(p0.at[rows_at(up), cols], r2.at[0], zp)
        hop_down[way].wait_recv()
        sum_at(down, cols, r1.at[1], first=HALF, count=HALF)
        end_down[way] = send(p0.at[rows_at(down), cols], r2.at[1], zm)

    finish(E_RIGHT, [7])
    finish(E_LEFT, [7])
    to_partner(2)
    first_hop(1, PLACE[1, 2], b, r1_b.at[1])
    finish(C, [5, 6, 7])
    part_over[PLACE[0, 2]].wait_recv()
    first_hop(0, PLACE[0, 2], b, r1_b.at[0])
    to_partner(1)
    to_partner(3)
    second_hop(1, PLACE[1, 1], PLACE[1, 3], b, r1_b.at[1], r2_b.at[1])
    finish(B, [5, 6, 7])
    finish(A, [5, 6, 7])
    to_partner(0)
    part_over[PLACE[0, 1]].wait_recv()
    part_over[PLACE[0, 3]].wait_recv()
    second_hop(0, PLACE[0, 1], PLACE[0, 3], b, r1_b.at[0], r2_b.at[0])
    x_first[2].wait_recv()
    first_hop(2, PLACE[0, 2], a, r1_a, xf.at[2])
    end_up[1].wait_recv()
    end_down[1].wait_recv()
    sum_at(1, b, s.at[1, :, b], r2_b.at[1, 0], r2_b.at[1, 1])
    last = send(p0.at[rows_at(1), b], xb, x2)
    x_first[1].wait_recv()
    x_first[3].wait_recv()
    second_hop(2, PLACE[0, 1], PLACE[0, 3], a, r1_a, r2_a, (xf.at[1],), (xf.at[3],))
    part_over[0].wait_recv()

    def renoise(cols, r2, partner):
        @pl.loop(0, ROWS // 16)
        def _(i):
            rows = pl.ds(pl.multiple_of(i * 16, 16), 16)
            mixed = p0[rows, cols].astype(jnp.float32) + s[0, rows, cols].astype(jnp.float32)
            mixed = mixed + r2[0, rows, :].astype(jnp.float32) + r2[1, rows, :].astype(jnp.float32)
            mixed = mixed + partner[rows, :].astype(jnp.float32)
            xrows = lat[rows, cols].astype(jnp.float32)
            fresh = noise[rows, cols].astype(jnp.float32)
            result = (1.0 - level_next) * (xrows - level_now * (xrows + mixed)) + level_next * fresh
            out[0, rows, cols] = result.astype(jnp.bfloat16)

    end_up[0].wait_recv()
    end_down[0].wait_recv()
    last.wait_recv()
    renoise(b, r2_b.at[0], xb)
    x_first[0].wait_recv()
    end_up[2].wait_recv()
    end_down[2].wait_recv()
    renoise(a, r2_a, xf.at[0])

    for copy in started:
        copy.wait_send()


def local(*operands):
    operands = operands[:9] + (operands[9].T,) + operands[10:]
    bf16, f32 = jnp.bfloat16, jnp.float32
    anywhere = pl.BlockSpec(memory_space=pl.ANY)
    vmem = pl.BlockSpec(memory_space=pltpu.VMEM)
    smem = pl.BlockSpec(memory_space=pltpu.SMEM)
    return pl.pallas_call(
        kernel,
        out_shape=jax.ShapeDtypeStruct((1, ROWS, D), bf16),
        in_specs=[anywhere] * 8 + [vmem] + [smem] * 4,
        out_specs=vmem,
        scratch_shapes=[
            pltpu.VMEM((ROWS, D), bf16),
            pltpu.VMEM((ROWS, D), bf16),
            pltpu.VMEM((3, D, W), bf16),
            pltpu.VMEM((W, D), bf16),
            pltpu.VMEM((TOK, D), bf16),
            pltpu.VMEM((9, 2, TOK, W), bf16),
            pltpu.VMEM((TOK, W), bf16),
            pltpu.VMEM((TOK, 2 * W), f32),
            pltpu.VMEM((TOK, W), f32),
            pltpu.VMEM((2 * 2 * ROWS, W), bf16),
            pltpu.VMEM((8, ROWS, D), bf16),
            pltpu.VMEM((2, HALF, X_COLS), bf16),
            pltpu.VMEM((2, 2, HALF, D - X_COLS), bf16),
            pltpu.VMEM((2, ROWS, X_COLS), bf16),
            pltpu.VMEM((2, 2, ROWS, D - X_COLS), bf16),
            pltpu.VMEM((4, ROWS, X_COLS), bf16),
            pltpu.VMEM((ROWS, D - X_COLS), bf16),
            pltpu.SMEM((16,), jnp.int32),
            pltpu.SemaphoreType.DMA((8,)),
            pltpu.SemaphoreType.DMA((N_SEM,)),
            pltpu.SemaphoreType.DMA((N_SEM,)),
        ],
        compiler_params=pltpu.CompilerParams(
            collective_id=0, has_side_effects=True, vmem_limit_bytes=62 * 2**20
        ),
    )(*operands)


def solution(mesh):
    in_specs = (
        P("span", "seq", None),
        P("span", "seq", None),
        P("span", None, "seq"),
        P("span", None, "seq"),
        P(None, "seq"),
        P(None, "seq"),
        P(None, "seq"),
        P("seq", None),
        P(),
        P(),
        P(),
        P(),
        P(),
    )
    out_specs = P("span", "seq", None)
    return jax.shard_map(local, mesh=mesh, in_specs=in_specs, out_specs=out_specs, check_vma=False)
```
